32 devices in a mesh: dp: 8 (over y, x, core), ctx: 4 (over z).
Axes of the slice: x: 2, y: 2, z: 4, core: 2. Of those that a mesh axis runs over, the one named last changes fastest.
Arguments:
- tokens: bfloat16 [8, 1024, 2048], P('dp', 'ctx'), may hold values from -6 to 6
- cotangent: bfloat16 [8, 1024, 2048], P('dp', 'ctx'), may hold values from -6 to 6
- qkv_weight: bfloat16 [2048, 6144], P(('dp', 'ctx')), may hold values from -0.125 to 0.125
- out_weight: bfloat16 [2048, 2048], P(('dp', 'ctx')), may hold values from -0.375 to 0.375
- up_weight: bfloat16 [2048, 8192], P(('dp', 'ctx')), may hold values from -0.125 to 0.125
- down_weight: bfloat16 [8192, 2048], P(('dp', 'ctx')), may hold values from -0.0625 to 0.0625
- vectors: bfloat16 [12, 2048], P(None, ('dp', 'ctx')), may hold values from -0.5 to 1.65, as said below
- qkv_moments: float32 [2, 2048, 6144], P(None, ('dp', 'ctx')), may hold values from -0.02 to 0.02, as said below
- out_moments: float32 [2, 2048, 2048], P(None, ('dp', 'ctx')), may hold values from -0.02 to 0.02, as said below
- up_moments: float32 [2, 2048, 8192], P(None, ('dp', 'ctx')), may hold values from -0.02 to 0.02, as said below
- down_moments: float32 [2, 8192, 2048], P(None, ('dp', 'ctx')), may hold values from -0.02 to 0.02, as said below
- vector_moments: float32 [2, 12, 2048], P(None, None, ('dp', 'ctx')), may hold values from -0.02 to 0.02, as said below
- step: int32 [], replicated, may hold values from 1 to 20
- hyper: float32 [5], replicated, may hold values from 0.002 to 200, as said below
Outputs:
- activations: bfloat16 [8, 1024, 2048], P('dp', 'ctx')
- input_grad: bfloat16 [8, 1024, 2048], P('dp', 'ctx')
- grad_norm: float32 [], replicated
- new_qkv_weight: bfloat16 [2048, 6144], P(('dp', 'ctx'))
- out_step: float32 [2048, 2048], P(('dp', 'ctx'))
- new_up_weight: bfloat16 [2048, 8192], P(('dp', 'ctx'))
- new_down_weight: bfloat16 [8192, 2048], P(('dp', 'ctx'))
- vector_step: float32 [12, 2048], P(None, ('dp', 'ctx'))
- new_qkv_moments: float32 [2, 2048, 6144], P(None, ('dp', 'ctx'))
- new_out_moments: float32 [2, 2048, 2048], P(None, ('dp', 'ctx'))
- new_up_moments: float32 [2, 2048, 8192], P(None, ('dp', 'ctx'))
- new_down_moments: float32 [2, 8192, 2048], P(None, ('dp', 'ctx'))
- new_vector_moments: float32 [2, 12, 2048], P(None, None, ('dp', 'ctx'))
The draws below stay inside these ranges and needn't reach their ends.
Inputs may be any that keep to these rules, and one draw needn't show every extreme that they name: `vectors`: rows 0 and 5 are positive gains, the others biases. `qkv_moments`: entry 0 of the first dimension is a first moment, entry 1 a positive second moment. `out_moments`: entry 0 of the first dimension is a first moment, entry 1 a positive second moment. `up_moments`: entry 0 of the first dimension is a first moment, entry 1 a positive second moment. `down_moments`: entry 0 of the first dimension is a first moment, entry 1 a positive second moment. `vector_moments`: entry 0 of the first dimension is a first moment, entry 1 a positive second moment. `hyper`: rate in 0.002 to 0.004, decay 0.05 to 0.2, first decay 0.85 to 0.95, second 0.95 to 0.999, clip maximum 50 to 200.
All inputs are finite; a program needn't handle non-finite values.
Results may differ from the reference program's by a relative error of at most 0.0095.
Values may be sent and summed in bfloat16 or wider, within the bound.
No kernel may reach another device: no remote copies, remote signals or barrier semaphores. Data moves between devices by JAX's collectives and lax.ppermute only.
A program may use at most 576 MiB of HBM per device.

```python
import math
import jax
import jax.numpy as jnp
from jax import lax

D = 2048
FF = 8192
HEADS = 16
HEAD_DIM = 128
BLOCK = 256
LENGTH = 1024
SEQS = 8


def moment_pair(key, row_count, col_count):
    first_moment = 0.02 * jax.random.uniform(jax.random.fold_in(key, 11), (row_count, col_count), jnp.float32, -1.0, 1.0)
    second_moment = jnp.exp(jax.random.uniform(jax.random.fold_in(key, 12), (row_count, col_count), jnp.float32, math.log(1e-05), math.log(0.001)))
    return jnp.stack([first_moment, second_moment])


def draw_qkv_moments(key, part):
    return moment_pair(key, D, 3 * D)


def draw_out_moments(key, part):
    return moment_pair(key, D, D)


def draw_up_moments(key, part):
    return moment_pair(key, D, FF)


def draw_down_moments(key, part):
    return moment_pair(key, FF, D)


def draw_vector_moments(key, part):
    return moment_pair(key, 12, D)


def draw_vectors(key, part):
    start_level = math.log(0.45)
    end_level = math.log(1.4)
    place = jnp.arange(D, dtype=jnp.int32).astype(jnp.float32) / float(max(D - 1, 1))
    ramp = start_level + (end_level - start_level) * place
    jitter = jax.random.uniform(jax.random.fold_in(key, 21), (12, D), jnp.float32, -0.15, 0.15)
    gains = jnp.exp(ramp[None, :] + jitter)
    shifts = jax.random.uniform(jax.random.fold_in(key, 22), (12, D), jnp.float32, -0.5, 0.5)
    row_ids = jnp.arange(12, dtype=jnp.int32)[:, None]
    return jnp.where((row_ids == 0) | (row_ids == 5), gains, shifts).astype(jnp.bfloat16)


def draw_hyper(key, part):
    low_ends = jnp.array([0.002, 0.05, 0.85, 0.95, 50.0], jnp.float32)
    high_ends = jnp.array([0.004, 0.2, 0.95, 0.999, 200.0], jnp.float32)
    return low_ends + (high_ends - low_ends) * jax.random.uniform(jax.random.fold_in(key, 31), (5,), jnp.float32)


def steps_of(rng, shape, pieces, smallest, top_value):
    loudness = 1.0
    for dim, shards_of in pieces:
        heights = jax.random.uniform(jax.random.fold_in(jax.random.fold_in(rng, 6), dim), (shards_of,), jnp.float32, smallest / len(pieces), top_value / len(pieces))
        loudness = loudness * jnp.repeat(jnp.exp(heights), shape[dim] // shards_of).reshape((-1,) + (1,) * (len(shape) - 1 - dim))
    return loudness


def bell_draw(own_key, extent, spread, most, pieces=(), held_as=jnp.bfloat16):
    drawn = spread * jax.random.normal(own_key, extent, jnp.float32)
    if pieces:
        drawn = drawn * steps_of(own_key, extent, pieces, -0.22, 0.18)
    return jnp.clip(drawn, -most, most).astype(held_as)


def setup_inputs(seed: int = 0) -> dict:
    arg_keys = jax.random.split(jax.random.key(seed), 15)
    return {
        "tokens": bell_draw(arg_keys[0], (SEQS, LENGTH, D), 1.0, 6.0, ((0, 8), (1, 4))),
        "cotangent": bell_draw(arg_keys[1], (SEQS, LENGTH, D), 1.0, 6.0, ((0, 8), (1, 4))),
        "qkv_weight": bell_draw(arg_keys[2], (D, 3 * D), D ** -0.5, 0.125, ((0, 32),)),
        "out_weight": bell_draw(arg_keys[3], (D, D), (D // 8) ** -0.5, 0.375, ((0, 32),)),
        "up_weight": bell_draw(arg_keys[4], (D, FF), D ** -0.5, 0.125, ((0, 32),)),
        "down_weight": bell_draw(arg_keys[5], (FF, D), FF ** -0.5, 0.0625, ((0, 32),)),
        "vectors": draw_vectors(jax.random.fold_in(arg_keys[14], 71), 0),
        "qkv_moments": draw_qkv_moments(jax.random.fold_in(arg_keys[14], 71), 0),
        "out_moments": draw_out_moments(jax.random.fold_in(arg_keys[14], 71), 0),
        "up_moments": draw_up_moments(jax.random.fold_in(arg_keys[14], 71), 0),
        "down_moments": draw_down_moments(jax.random.fold_in(arg_keys[14], 71), 0),
        "vector_moments": draw_vector_moments(jax.random.fold_in(arg_keys[14], 71), 0),
        "step": jax.random.randint(arg_keys[12], (), 1, 21).astype(jnp.int32),
        "hyper": draw_hyper(jax.random.fold_in(arg_keys[14], 71), 0),
    }


EPS_NORM = 1e-05
EPS_ADAM = 1e-08
MASKED = -1e+30
HIGHEST = lax.Precision.HIGHEST

@jax.custom_vjp
def low(v):
    return lax.optimization_barrier(v.astype(jnp.bfloat16)).astype(jnp.float32)

@jax.custom_vjp
def low_back(v):
    return v

def low_keep(v):
    return (low(v), None)

def low_pass(kept, grad):
    return (grad,)

def back_keep(v):
    return (v, None)

def back_low(kept, grad):
    return (low(grad),)
low.defvjp(low_keep, low_pass)
low_back.defvjp(back_keep, back_low)

def layer_norm(values, gain, shift):
    centre = values - lax.optimization_barrier(jnp.mean(values, axis=-1, keepdims=True))
    factor = lax.rsqrt(lax.optimization_barrier(jnp.mean(centre * centre, axis=-1, keepdims=True)) + EPS_NORM)
    return centre * factor * gain + shift

def attend(queries, keys, values):
    length = queries.shape[0]
    head_count = queries.shape[1]
    position = jnp.arange(length, dtype=jnp.int32)
    slopes = jnp.exp2(-8.0 * (jnp.arange(head_count).astype(jnp.float32) + 1.0) / head_count)
    distance = jnp.abs(position[:, None] - position[None, :]).astype(jnp.float32)
    allowed = position[None, :] // BLOCK <= position[:, None] // BLOCK
    scores = jnp.einsum('qhe,khe->hqk', queries, keys, precision=HIGHEST) * HEAD_DIM ** (-0.5)
    scores = scores - slopes[:, None, None] * distance[None]
    scores = jnp.where(allowed[None], scores, MASKED)
    scores = low_back(scores)
    probs = low(jax.nn.softmax(scores, axis=-1))
    return jnp.einsum('hqk,khe->qhe', probs, values, precision=HIGHEST)

def forward(block_in, w_qkv, w_out, w_up, w_down, vecs):
    group, length, width = block_in.shape
    rows_in = block_in.reshape(group * length, width)
    normed_a = low(layer_norm(rows_in, vecs[0], vecs[1]))
    qkv = jnp.dot(normed_a, w_qkv, precision=HIGHEST, preferred_element_type=jnp.float32)
    queries = low_back(low(qkv[:, :width] + vecs[2]))
    keys = low_back(low(qkv[:, width:2 * width]))
    values = low_back(low(qkv[:, 2 * width:] + vecs[3]))
    shape_heads = (group, length, HEADS, HEAD_DIM)
    context = lax.map(jax.checkpoint(lambda triple: attend(triple[0], triple[1], triple[2])), (queries.reshape(shape_heads), keys.reshape(shape_heads), values.reshape(shape_heads)))
    context = low_back(low(context.reshape(group * length, width)))
    attn_out = low_back(jnp.dot(context, w_out, precision=HIGHEST, preferred_element_type=jnp.float32) + vecs[4])
    residual = rows_in + attn_out
    normed_b = low(layer_norm(residual, vecs[5], vecs[6]))
    up_bias = vecs[8:12].reshape(-1)
    pre_act = low_back(jnp.dot(normed_b, w_up, precision=HIGHEST, preferred_element_type=jnp.float32) + up_bias)
    hidden = low(jax.nn.gelu(pre_act, approximate=True))
    mlp_out = low_back(jnp.dot(hidden, w_down, precision=HIGHEST, preferred_element_type=jnp.float32) + vecs[7])
    return (residual + mlp_out).reshape(group, length, width)

def adam_update(weight, moments, grad, clip_factor, step, hyper):
    step_float = step.astype(jnp.float32)
    scaled = grad * clip_factor
    first_moment = hyper[2] * moments[0] + (1.0 - hyper[2]) * scaled
    second_moment = hyper[3] * moments[1] + (1.0 - hyper[3]) * scaled * scaled
    fix_first = 1.0 - hyper[2] ** step_float
    fix_second = 1.0 - hyper[3] ** step_float
    current = weight.astype(jnp.float32)
    change = -hyper[0] * (first_moment / fix_first / (jnp.sqrt(second_moment / fix_second) + EPS_ADAM) + hyper[1] * current)
    updated = current + change
    return (updated.astype(jnp.bfloat16), change, jnp.stack([first_moment, second_moment]))

def reference(tokens, cotangent, qkv_weight, out_weight, up_weight, down_weight, vectors, qkv_moments, out_moments, up_moments, down_moments, vector_moments, step, hyper):
    weights = tuple((item.astype(jnp.float32) for item in (qkv_weight, out_weight, up_weight, down_weight, vectors)))
    group = 4 if SEQS % 4 == 0 else 2 if SEQS % 2 == 0 else 1
    inputs = tokens.astype(jnp.float32).reshape(SEQS // group, group, LENGTH, D)
    cotans = cotangent.astype(jnp.float32).reshape(SEQS // group, group, LENGTH, D)

    def one_group(carry, item):
        block_in, block_cot = item
        result, pull = jax.vjp(forward, block_in, *weights)
        grads = pull(block_cot)
        summed = tuple((acc + new for acc, new in zip(carry, grads[1:])))
        return (summed, (result.astype(jnp.bfloat16), grads[0].astype(jnp.bfloat16)))
    zeros = tuple((jnp.zeros(item.shape, jnp.float32) for item in weights))
    totals, (outs_y, outs_dx) = lax.scan(one_group, zeros, (inputs, cotans))
    squares = jnp.float32(0.0)
    for grad in totals:
        squares = squares + jnp.sum(grad * grad)
    grad_norm = jnp.sqrt(squares)
    clip_factor = jnp.minimum(1.0, hyper[4] / (grad_norm + 1e-06))
    moments = (qkv_moments, out_moments, up_moments, down_moments, vector_moments)
    news = [adam_update(w, m, g, clip_factor, step, hyper) for w, m, g in zip((qkv_weight, out_weight, up_weight, down_weight, vectors), moments, totals)]
    return (outs_y.reshape(SEQS, LENGTH, D), outs_dx.reshape(SEQS, LENGTH, D), grad_norm, news[0][0], news[1][1], news[2][0], news[3][0], news[4][1], news[0][2], news[1][2], news[2][2], news[3][2], news[4][2])
```

```python
from functools import partial

import jax
import jax.numpy as jnp
import numpy as np
from jax import lax
from jax.experimental import pallas as pl
from jax.experimental.pallas import tpu as pltpu
from jax.sharding import Mesh
from jax.sharding import PartitionSpec as P

HEADS = 16
HEAD_DIM = 128
GROUP = 8
CHIPS = GROUP // 2

EPS_NORM = 1e-05
EPS_ADAM = 1e-08
F32 = jnp.float32
BF16 = jnp.bfloat16
AXES = ("o", "p", "z")
VMEM_LIMIT = 56 * 1024 * 1024


def dot(a, b):
    return jnp.dot(a, b, preferred_element_type=F32)


def dot_nt(a, b):
    return lax.dot_general(a, b, (((1,), (1,)), ((), ())), preferred_element_type=F32)


def dot_tn(a, b):
    return lax.dot_general(a, b, (((0,), (0,)), ((), ())), preferred_element_type=F32)


def permute(value, target):
    sizes = [lax.axis_size(a) for a in AXES]
    pairs = []
    for o in range(sizes[0]):
        for p in range(sizes[1]):
            for z in range(sizes[2]):
                to = target(o, p, z)
                flat = lambda c: (c[0] * sizes[1] + c[1]) * sizes[2] + c[2]
                pairs.append((flat((o, p, z)), flat(to)))
    return lax.ppermute(value, AXES, pairs)


def swap_p(value, k):
    return permute(value, lambda o, p, z: (o, p ^ k, z))


def swap_z(value, k):
    return permute(value, lambda o, p, z: (o, p, z ^ k))


def swap_o(value, k):
    return permute(value, lambda o, p, z: (o ^ k, p, z))


def sum_all(value):
    for swap, size in ((swap_p, GROUP), (swap_z, lax.axis_size("z")), (swap_o, lax.axis_size("o"))):
        k = 1
        while k < size:
            value = value + swap(value, k)
            k *= 2
    return value


def pick(stacked, index):
    return lax.dynamic_index_in_dim(stacked, index, 0, keepdims=False)


def spread(block, chip, z):
    rows = block.shape[0] // CHIPS
    parts = block.reshape(CHIPS, rows, block.shape[1])
    held = [pick(parts, chip)]
    for k in range(1, CHIPS):
        held.append(swap_p(pick(parts, chip ^ k), 2 * k))
    held = jnp.stack(held)
    arrived = [pick(held, chip ^ z)]
    for j in range(1, CHIPS):
        arrived.append(swap_z(pick(held, chip ^ z ^ j), j))
    return jnp.concatenate(arrived, axis=0)


def unspread(block, chip, z):
    rows = block.shape[0] // CHIPS
    parts = block.reshape(CHIPS, rows, block.shape[1])
    held = [parts[0]]
    for j in range(1, CHIPS):
        held.append(swap_z(parts[j], j))
    held = jnp.stack(held)
    arrived = [pick(held, chip ^ z)]
    for k in range(1, CHIPS):
        arrived.append(swap_p(pick(held, chip ^ k ^ z), 2 * k))
    arrived = jnp.stack(arrived)
    return jnp.concatenate([pick(arrived, q ^ chip) for q in range(CHIPS)], axis=0)


def plane_gather(block):
    own = [block] + [swap_p(block, 2 * k) for k in range(1, CHIPS)]
    other = [swap_p(v, 1) for v in own]
    return [jnp.concatenate(own, axis=0), jnp.concatenate(other, axis=0)]


def plane_reduce(own_terms, other_terms):
    rows = own_terms.shape[0] // CHIPS
    total = None
    for k in range(CHIPS):
        span = slice(k * rows, (k + 1) * rows)
        part = own_terms[span].astype(F32) + swap_p(other_terms[span], 1).astype(F32)
        if k:
            part = swap_p(part.astype(BF16), 2 * k).astype(F32)
        total = part if total is None else total + part
    return total


def gather_columns(weight, groups):
    rows, cols = weight.shape
    width = cols // (groups * GROUP)
    parts = weight.reshape(rows, groups, GROUP, width).transpose(2, 0, 1, 3)
    parts = parts.reshape(GROUP, rows, groups * width)
    parts = lax.all_to_all(parts, "p", 0, 0, tiled=True)
    full = lax.all_gather(parts, ("o", "z"), axis=0, tiled=False)
    o_size, z_size = lax.axis_size("o"), lax.axis_size("z")
    full = full.reshape(o_size, z_size, GROUP, rows, groups * width).transpose(0, 2, 1, 3, 4)
    return full.reshape(-1, groups * width)


def scatter_columns(grad, groups, rows):
    o_size, z_size = lax.axis_size("o"), lax.axis_size("z")
    width = grad.shape[1] // groups
    parts = grad.reshape(o_size, GROUP, z_size, rows, -1).transpose(0, 2, 1, 3, 4)
    parts = parts.reshape(-1, groups * width)
    mine = lax.psum_scatter(parts, ("o", "z"), scatter_dimension=0, tiled=True)
    mine = lax.all_to_all(mine, "p", 0, 0, tiled=True)
    mine = mine.reshape(GROUP, rows, groups, width).transpose(1, 2, 0, 3)
    return mine.reshape(rows, -1).astype(F32)


def gather_rows(weight, p):
    if lax.axis_size("o") == 1:
        return lax.all_gather(weight, "z", axis=0, tiled=True)
    full = lax.all_gather(weight, AXES, axis=0, tiled=True)
    return pick(full.reshape(GROUP, -1, weight.shape[1]), p)


def scatter_rows(grad, p):
    if lax.axis_size("o") == 1:
        return lax.psum_scatter(grad, "z", scatter_dimension=0, tiled=True).astype(F32)
    full = jnp.zeros((GROUP,) + grad.shape, grad.dtype)
    full = lax.dynamic_update_index_in_dim(full, grad, p, 0)
    full = full.reshape(-1, grad.shape[1])
    return lax.psum_scatter(full, AXES, scatter_dimension=0, tiled=True).astype(F32)


def order_rows(pos_ref, blocks, rows):
    out = []
    for b in range(blocks):
        for q in range(CHIPS):
            held = ((q ^ pos_ref[0]) * blocks + (b ^ pos_ref[1])) * rows
            out.append(((b * CHIPS + q) * rows, pl.multiple_of(held, rows)))
    return out


def block_probs(q, keys, slope, start, scale):
    scores = dot_nt(q, keys) * scale
    row = lax.broadcasted_iota(jnp.int32, scores.shape, 0) + start
    col = lax.broadcasted_iota(jnp.int32, scores.shape, 1)
    scores = scores - slope * jnp.abs(row - col).astype(F32)
    expo = jnp.exp(scores - jnp.max(scores, axis=-1, keepdims=True))
    return expo * (1.0 / jnp.sum(expo, axis=-1, keepdims=True))


def attend_kernel(blocks, scale, pos_ref, slope_ref, q_ref, k_ref, v_ref, ctx_ref, qs, ks, vs):
    rows = q_ref.shape[0] // (blocks * CHIPS)
    block = rows * CHIPS
    slope = slope_ref[pl.program_id(0)]
    order = order_rows(pos_ref, blocks, rows)
    for nat, held in order:
        qs[nat : nat + rows] = q_ref[pl.ds(held, rows), :]
        ks[nat : nat + rows] = k_ref[pl.ds(held, rows), :]
        vs[nat : nat + rows] = v_ref[pl.ds(held, rows), :]
    for b in range(blocks):
        end = (b + 1) * block
        probs = block_probs(qs[b * block : end], ks[:end], slope, b * block, scale)
        ctx = dot(probs.astype(BF16), vs[:end]).astype(BF16)
        for q in range(CHIPS):
            held = order[b * CHIPS + q][1]
            ctx_ref[pl.ds(held, rows), :] = ctx[q * rows : (q + 1) * rows]


def attend_back_kernel(
    blocks, scale, pos_ref, slope_ref, q_ref, k_ref, v_ref, g_ref, gq_ref, gk_ref, gv_ref,
    qs, ks, vs, gs, gks, gvs,
):
    rows = q_ref.shape[0] // (blocks * CHIPS)
    block = rows * CHIPS
    slope = slope_ref[pl.program_id(0)]
    order = order_rows(pos_ref, blocks, rows)
    for nat, held in order:
        qs[nat : nat + rows] = q_ref[pl.ds(held, rows), :]
        ks[nat : nat + rows] = k_ref[pl.ds(held, rows), :]
        vs[nat : nat + rows] = v_ref[pl.ds(held, rows), :]
        gs[nat : nat + rows] = g_ref[pl.ds(held, rows), :]
    for b in reversed(range(blocks)):
        start, end = b * block, (b + 1) * block
        q, g = qs[start:end], gs[start:end]
        keys, values = ks[:end], vs[:end]
        probs = block_probs(q, keys, slope, start, scale)
        grad_values = dot_tn(probs.astype(BF16), g)
        grad_probs = dot_nt(g, values)
        inner = jnp.sum(probs * grad_probs, axis=-1, keepdims=True)
        grad_scores = (probs * (grad_probs - inner)).astype(BF16)
        grad_q = (dot(grad_scores, keys) * scale).astype(BF16)
        grad_keys = dot_tn(grad_scores, q)
        if b == blocks - 1:
            gks[...] = grad_keys
            gvs[...] = grad_values
        else:
            gks[:end] += grad_keys
            gvs[:end] += grad_values
        for c in range(CHIPS):
            held = order[b * CHIPS + c][1]
            gq_ref[pl.ds(held, rows), :] = grad_q[c * rows : (c + 1) * rows]
    for nat, held in order:
        gk_ref[pl.ds(held, rows), :] = (gks[nat : nat + rows] * scale).astype(BF16)
        gv_ref[pl.ds(held, rows), :] = gvs[nat : nat + rows].astype(BF16)


def attend(qkv, place, slopes):
    length, heads = qkv.shape[0], qkv.shape[1] // (3 * HEAD_DIM)
    blocks = lax.axis_size("z")
    smem = pl.BlockSpec(memory_space=pltpu.SMEM)
    column = lambda first: pl.BlockSpec((length, HEAD_DIM), lambda h: (0, first + h))
    held = pltpu.VMEM((length, HEAD_DIM), BF16)
    return pl.pallas_call(
        partial(attend_kernel, blocks, HEAD_DIM**-0.5),
        grid=(heads,),
        in_specs=[smem, smem, column(0), column(heads), column(2 * heads)],
        out_specs=column(0),
        out_shape=jax.ShapeDtypeStruct((length, heads * HEAD_DIM), BF16),
        scratch_shapes=[held] * 3,
        compiler_params=pltpu.CompilerParams(vmem_limit_bytes=VMEM_LIMIT),
        cost_estimate=pl.CostEstimate(
            flops=3 * length * length * HEAD_DIM * heads,
            bytes_accessed=8 * length * heads * HEAD_DIM,
            transcendentals=length * length * heads,
        ),
    )(place, slopes, qkv, qkv, qkv)


def attend_back(qkv, grad_ctx, place, slopes):
    length, heads = qkv.shape[0], qkv.shape[1] // (3 * HEAD_DIM)
    blocks = lax.axis_size("z")
    smem = pl.BlockSpec(memory_space=pltpu.SMEM)
    column = lambda first: pl.BlockSpec((length, HEAD_DIM), lambda h: (0, first + h))
    held = pltpu.VMEM((length, HEAD_DIM), BF16)
    wide = pltpu.VMEM((length, HEAD_DIM), F32)
    return pl.pallas_call(
        partial(attend_back_kernel, blocks, HEAD_DIM**-0.5),
        grid=(heads,),
        in_specs=[smem, smem, column(0), column(heads), column(2 * heads), column(0)],
        out_specs=[column(0)] * 3,
        out_shape=[jax.ShapeDtypeStruct((length, heads * HEAD_DIM), BF16)] * 3,
        scratch_shapes=[held] * 4 + [wide] * 2,
        compiler_params=pltpu.CompilerParams(vmem_limit_bytes=VMEM_LIMIT),
        cost_estimate=pl.CostEstimate(
            flops=8 * length * length * HEAD_DIM * heads,
            bytes_accessed=14 * length * heads * HEAD_DIM,
            transcendentals=length * length * heads,
        ),
    )(place, slopes, qkv, qkv, qkv, grad_ctx)


def norm_forward(values, gain, shift):
    centre = values - jnp.mean(values, axis=-1, keepdims=True)
    factor = lax.rsqrt(jnp.mean(centre * centre, axis=-1, keepdims=True) + EPS_NORM)
    normed = centre * factor
    return (normed * gain + shift, normed, factor)


def norm_backward(incoming, normed, factor, gain):
    scaled = incoming * gain
    input_grad = factor * (
        scaled
        - jnp.mean(scaled, axis=-1, keepdims=True)
        - normed * jnp.mean(scaled * normed, axis=-1, keepdims=True)
    )
    return (input_grad, jnp.sum(incoming * normed, axis=0), jnp.sum(incoming, axis=0))


def adam_update(weight, moments, grad, clip_factor, step, hyper):
    step_float = step.astype(F32)
    scaled = grad * clip_factor
    first_moment = hyper[2] * moments[0] + (1.0 - hyper[2]) * scaled
    second_moment = hyper[3] * moments[1] + (1.0 - hyper[3]) * scaled * scaled
    fix_first = 1.0 - hyper[2] ** step_float
    fix_second = 1.0 - hyper[3] ** step_float
    current = weight.astype(F32)
    change = -hyper[0] * (
        first_moment / fix_first / (jnp.sqrt(second_moment / fix_second) + EPS_ADAM)
        + hyper[1] * current
    )
    updated = current + change
    return (updated.astype(BF16), change, jnp.stack([first_moment, second_moment]))


def column_sum(values):
    return jnp.sum(values.astype(F32), axis=0)


def body(
    tokens,
    cotangent,
    qkv_weight,
    out_weight,
    up_weight,
    down_weight,
    vectors,
    qkv_moments,
    out_moments,
    up_moments,
    down_moments,
    vector_moments,
    step,
    hyper,
):
    o, p, z = (lax.axis_index(a) for a in AXES)
    chip = p >> 1
    width = tokens.shape[2]
    place = jnp.stack([chip, z]).astype(jnp.int32)
    heads = HEADS // GROUP
    head_ids = (p * heads + jnp.arange(heads)).astype(F32)
    slopes = jnp.exp2(-8.0 * (head_ids + 1.0) / HEADS)
    tokens_given, top_given = tokens[0], cotangent[0]

    w_qkv = gather_columns(qkv_weight, 3)
    rows_low = spread(tokens_given, chip, z)
    flat = (o * GROUP + p) * lax.axis_size("z") + z
    vec_cols = vectors.shape[1]
    vec_low = lax.dynamic_update_slice(
        jnp.zeros((vectors.shape[0], width), BF16), vectors, (0, flat * vec_cols)
    )
    vecs = sum_all(vec_low).astype(F32)
    w_out = gather_rows(out_weight, p)
    w_up = gather_columns(up_weight, 1)
    w_down = gather_rows(down_weight, p)
    top_low = spread(top_given, chip, z)

    rows_in = rows_low.astype(F32)
    normed, hat_one, factor_one = norm_forward(rows_in, vecs[0], vecs[1])
    normed_a = plane_gather(normed.astype(BF16))
    part = width // GROUP
    bias_q = lax.dynamic_slice(vecs[2], (p * part,), (part,))
    bias_v = lax.dynamic_slice(vecs[3], (p * part,), (part,))
    bias_qkv = jnp.concatenate([bias_q, jnp.zeros_like(bias_q), bias_v])
    qkv = [(dot(v, w_qkv) + bias_qkv).astype(BF16) for v in normed_a]
    context = [attend(v, place, slopes) for v in qkv]
    attn = plane_reduce(*[dot(v, w_out).astype(BF16) for v in context])
    residual = rows_in + attn + vecs[4]
    normed, hat_two, factor_two = norm_forward(residual, vecs[5], vecs[6])
    normed_b = plane_gather(normed.astype(BF16))
    hidden_part = w_up.shape[1]
    bias_up = lax.dynamic_slice(vecs[8:].reshape(-1), (p * hidden_part,), (hidden_part,))
    pre_act = [dot(v, w_up) + bias_up for v in normed_b]
    hidden = [jax.nn.gelu(v, approximate=True).astype(BF16) for v in pre_act]
    mlp = plane_reduce(*[dot(v, w_down).astype(BF16) for v in hidden])
    activations = unspread((residual + mlp + vecs[7]).astype(BF16), chip, z)

    grad_top = top_low.astype(F32)
    grad_mlp = plane_gather(top_low)
    grad_down = dot_tn(hidden[0], grad_mlp[0]) + dot_tn(hidden[1], grad_mlp[1])
    owned_down = scatter_rows(grad_down.astype(BF16), p)
    grad_pre = []
    for v, g in zip(pre_act, grad_mlp):
        _, pull = jax.vjp(partial(jax.nn.gelu, approximate=True), v)
        grad_pre.append(pull(dot_nt(g, w_down))[0].astype(BF16))
    grad_up = dot_tn(normed_b[0], grad_pre[0]) + dot_tn(normed_b[1], grad_pre[1])
    owned_up = scatter_columns(grad_up.astype(BF16), 1, up_weight.shape[0])
    grad_normed = plane_reduce(*[dot_nt(g, w_up).astype(BF16) for g in grad_pre])
    through, gain_two_grad, shift_two_grad = norm_backward(grad_normed, hat_two, factor_two, vecs[5])
    grad_residual = grad_top + through
    grad_attn_own = grad_residual.astype(BF16)
    grad_attn = plane_gather(grad_attn_own)
    grad_context = [dot_nt(g, w_out).astype(BF16) for g in grad_attn]
    grad_out = dot_tn(context[0], grad_attn[0]) + dot_tn(context[1], grad_attn[1])
    owned_out = scatter_rows(grad_out.astype(BF16), p)
    grads = [attend_back(v, g, place, slopes) for v, g in zip(qkv, grad_context)]
    grad_qkv = [jnp.concatenate(g, axis=1) for g in grads]
    grad_qkv_weight = dot_tn(normed_a[0], grad_qkv[0]) + dot_tn(normed_a[1], grad_qkv[1])
    owned_qkv = scatter_columns(grad_qkv_weight.astype(BF16), 3, qkv_weight.shape[0])
    grad_normed = plane_reduce(*[dot_nt(g, w_qkv).astype(BF16) for g in grad_qkv])
    through, gain_one_grad, shift_one_grad = norm_backward(grad_normed, hat_one, factor_one, vecs[0])
    input_grad = unspread((grad_residual + through).astype(BF16), chip, z)

    bias_grads = column_sum(grad_qkv[0]) + column_sum(grad_qkv[1])
    up_bias_grad = column_sum(grad_pre[0]) + column_sum(grad_pre[1])
    wide = lambda v: lax.dynamic_update_slice(jnp.zeros((width,), F32), v, (p * part,))
    up_wide = lax.dynamic_update_slice(
        jnp.zeros((GROUP * hidden_part,), F32), up_bias_grad, (p * hidden_part,)
    )
    vector_grad = jnp.concatenate(
        [
            jnp.stack(
                [
                    gain_one_grad,
                    shift_one_grad,
                    wide(bias_grads[:part]),
                    wide(bias_grads[2 * part :]),
                    column_sum(grad_attn_own),
                    gain_two_grad,
                    shift_two_grad,
                    column_sum(top_given),
                ]
            ),
            up_wide.reshape(-1, width),
        ],
        axis=0,
    )
    owned_vec = lax.dynamic_slice(
        sum_all(vector_grad), (0, flat * vec_cols), (vectors.shape[0], vec_cols)
    )

    owned = (owned_qkv, owned_out, owned_up, owned_down, owned_vec)
    squares = sum(jnp.sum(g * g) for g in owned)
    grad_norm = jnp.sqrt(sum_all(squares.reshape(1, 1))[0, 0])
    clip_factor = jnp.minimum(1.0, hyper[4] / (grad_norm + 1e-06))
    shards = (qkv_weight, out_weight, up_weight, down_weight, vectors)
    moments = (qkv_moments, out_moments, up_moments, down_moments, vector_moments)
    news = [
        adam_update(w, m, g, clip_factor, step, hyper) for w, m, g in zip(shards, moments, owned)
    ]
    return (
        activations[None],
        input_grad[None],
        grad_norm,
        news[0][0],
        news[1][1],
        news[2][0],
        news[3][0],
        news[4][1],
        news[0][2],
        news[1][2],
        news[2][2],
        news[3][2],
        news[4][2],
    )


def solution(mesh):
    devices = np.asarray(mesh.devices)
    planes = Mesh(devices.reshape(-1, GROUP, devices.shape[1]), AXES)
    rows = P(AXES, None)
    seqs = P(("o", "p"), "z", None)
    pair = P(None, AXES, None)
    cols = P(None, AXES)
    return jax.shard_map(
        body,
        mesh=planes,
        in_specs=(seqs, seqs, rows, rows, rows, rows, cols)
        + (pair, pair, pair, pair, P(None, None, AXES), P(), P()),
        out_specs=(seqs, seqs, P(), rows, rows, rows, rows, cols)
        + (pair, pair, pair, pair, P(None, None, AXES)),
        check_vma=False,
    )
```

```python
from functools import partial

import jax
import jax.numpy as jnp
import numpy as np
from jax import lax
from jax.experimental import pallas as pl
from jax.experimental.pallas import tpu as pltpu
from jax.sharding import Mesh
from jax.sharding import PartitionSpec as P

HEADS = 16
HEAD_DIM = 128
GROUP = 8
CHIPS = GROUP // 2

EPS_NORM = 1e-05
EPS_ADAM = 1e-08
F32 = jnp.float32
BF16 = jnp.bfloat16
PLANE = ("chip", "core")
AXES = ("o",) + PLANE + ("z",)
VMEM_LIMIT = 56 * 1024 * 1024


def after(value, *others):
    return lax.optimization_barrier((value,) + others)[0]


def together(*values):
    return lax.optimization_barrier(values)


def dot(a, b):
    return jnp.dot(a, b, preferred_element_type=F32)


def dot_nt(a, b):
    return lax.dot_general(a, b, (((1,), (1,)), ((), ())), preferred_element_type=F32)


def dot_tn(a, b):
    return lax.dot_general(a, b, (((0,), (0,)), ((), ())), preferred_element_type=F32)


def swap_chips(value, k):
    return lax.ppermute(value, "chip", [(q, q ^ k) for q in range(CHIPS)])


def swap_cores(value):
    return lax.ppermute(value, "core", [(0, 1), (1, 0)])


def swap(value, axis, k):
    return lax.ppermute(value, axis, [(i, i ^ k) for i in range(lax.axis_size(axis))])


def sum_all(value):
    for axis in AXES:
        k = 1
        while k < lax.axis_size(axis):
            value = value + swap(value, axis, k)
            k *= 2
    return value


def trade(value, axes):
    return lax.all_to_all(value, axes, 0, 0, tiled=True)


def pick(stacked, index):
    return lax.dynamic_index_in_dim(stacked, index, 0, keepdims=False)


def plane_order(own):
    return [own] + [swap_chips(own, k) for k in range(1, CHIPS)]


def to_planes(parts):
    z = lax.axis_index("z")
    return [pick(parts, z)] + [swap(pick(parts, z ^ k), "z", k) for k in range(1, CHIPS)]


def in_z_order(natural):
    z = lax.axis_index("z")
    parts = natural.reshape(CHIPS, -1, natural.shape[1])
    return jnp.concatenate([pick(parts, z ^ k) for k in range(CHIPS)], axis=0)


def from_planes(block):
    parts = block.reshape(CHIPS, -1, block.shape[1])
    return [parts[0]] + [swap(parts[k], "z", k) for k in range(1, CHIPS)]


def to_owners(pieces):
    z = lax.axis_index("z")
    held = jnp.stack(pieces)
    return trade(jnp.concatenate([pick(held, z ^ q) for q in range(CHIPS)], axis=0), "chip")


def core_pieces(own_terms, other_terms):
    rows = own_terms.shape[0] // CHIPS
    arrived = swap_cores(other_terms)
    near = own_terms[:rows].astype(F32) + arrived[:rows].astype(F32)
    far = (own_terms[rows:].astype(F32) + arrived[rows:].astype(F32)).astype(BF16)
    return [near] + [far[k * rows : (k + 1) * rows] for k in range(CHIPS - 1)]


def chip_exchange(pieces):
    return pieces[:1] + [swap_chips(v, k) for k, v in enumerate(pieces) if k]


def add_up(pieces):
    return sum(v.astype(F32) for v in pieces)


def sum_parts(parts):
    return jnp.sum(parts.reshape(CHIPS, -1, parts.shape[1]).astype(F32), axis=0)


def chip_trade(pieces, chip):
    parts = jnp.stack([pieces[0].astype(BF16)] + pieces[1:])
    low = jnp.concatenate([pick(parts, chip ^ q) for q in range(CHIPS)], axis=0)
    return trade(low, "chip")


def trade_columns(weight, groups):
    rows, cols = weight.shape
    width = cols // (groups * GROUP)
    parts = weight.reshape(rows, groups, GROUP, width).transpose(2, 0, 1, 3)
    parts = parts.reshape(GROUP, rows, groups * width)
    return trade(parts, PLANE)


def side_by_side(stack, count):
    rows = stack.shape[0] // count
    return stack.reshape(count, rows, -1).transpose(1, 0, 2).reshape(rows, -1)


def stacked(wide, count):
    rows = wide.shape[0]
    return wide.reshape(rows, count, -1).transpose(1, 0, 2).reshape(count * rows, -1)


def in_row_order(full, width):
    o_size, z_size = lax.axis_size("o"), lax.axis_size("z")
    full = full.reshape(o_size, z_size, GROUP, -1, width).transpose(0, 2, 1, 3, 4)
    return full.reshape(-1, width)


def pair_up(parts, rows_weight, beside):
    width = parts.shape[2]
    flat = parts.reshape(-1, width)
    if lax.axis_size("o") > 1:
        return (flat, rows_weight)
    count = GROUP if beside else rows_weight.shape[1] // width
    return (jnp.concatenate([flat, after(stacked(rows_weight, count), ())], axis=1 if beside else 0),)


def gather_pair(pair, parts, rows_weight, p, beside):
    width = parts.shape[2]
    if len(pair) > 1:
        full = lax.all_gather(pair[0], ("o", "z"), axis=0, tiled=True)
        others = lax.all_gather(pair[1], AXES, axis=0, tiled=True)
        return in_row_order(full, width), pick(others.reshape(GROUP, -1, rows_weight.shape[1]), p)
    full = lax.all_gather(pair[0], "z", axis=0, tiled=False)
    first, second = jnp.split(full, [width if beside else parts.size // width], axis=2 if beside else 1)
    count = GROUP if beside else rows_weight.shape[1] // width
    second = [side_by_side(second[i], count) for i in range(full.shape[0])]
    return in_row_order(first, width), jnp.concatenate(second, axis=0)


def scatter_pair(grad_columns, grad_rows, rows, p):
    width = grad_columns.shape[1]
    if lax.axis_size("o") > 1:
        return scatter_columns(grad_columns), scatter_rows(grad_rows, p)
    z_size = lax.axis_size("z")
    beside = grad_rows.reshape(z_size, -1, grad_rows.shape[1])
    beside = after(jnp.concatenate([stacked(beside[i], GROUP) for i in range(z_size)], axis=0), ())
    both = jnp.concatenate([grad_columns, beside], axis=1)
    mine = lax.psum_scatter(both, "z", scatter_dimension=0, tiled=True)
    return mine[:, :width].reshape(GROUP, rows, width), side_by_side(mine[:, width:], GROUP)


def by_owner(grad, rows):
    o_size, z_size = lax.axis_size("o"), lax.axis_size("z")
    parts = grad.reshape(o_size, GROUP, z_size, rows, -1).transpose(0, 2, 1, 3, 4)
    return parts.reshape(grad.shape)


def scatter_columns(parts):
    mine = lax.psum_scatter(parts, ("o", "z"), scatter_dimension=0, tiled=True)
    return mine.reshape(GROUP, -1, parts.shape[1])


def trade_rows(parts):
    return trade(parts, PLANE)


def gather_rows(weight, p):
    if lax.axis_size("o") == 1:
        return lax.all_gather(weight, "z", axis=0, tiled=True)
    full = lax.all_gather(weight, AXES, axis=0, tiled=True)
    return pick(full.reshape(GROUP, -1, weight.shape[1]), p)


def scatter_rows(grad, p):
    if lax.axis_size("o") == 1:
        return lax.psum_scatter(grad, "z", scatter_dimension=0, tiled=True)
    full = jnp.zeros((GROUP,) + grad.shape, grad.dtype)
    full = lax.dynamic_update_index_in_dim(full, grad, p, 0)
    full = full.reshape(-1, grad.shape[1])
    return lax.psum_scatter(full, AXES, scatter_dimension=0, tiled=True)


def order_rows(pos_ref, blocks, rows):
    out = []
    for b in range(blocks):
        for q in range(CHIPS):
            held = ((q ^ pos_ref[0]) * blocks + (b ^ pos_ref[1])) * rows
            out.append(((b * CHIPS + q) * rows, pl.multiple_of(held, rows)))
    return out


def block_probs(q, keys, slope, start, scale):
    scores = dot_nt(q, keys) * scale
    row = lax.broadcasted_iota(jnp.int32, scores.shape, 0) + start
    col = lax.broadcasted_iota(jnp.int32, scores.shape, 1)
    scores = scores - slope * jnp.abs(row - col).astype(F32)
    expo = jnp.exp(scores - jnp.max(scores, axis=-1, keepdims=True))
    return expo * (1.0 / jnp.sum(expo, axis=-1, keepdims=True))


def attend_kernel(blocks, scale, pos_ref, slope_ref, q_ref, k_ref, v_ref, ctx_ref, qs, ks, vs):
    rows = q_ref.shape[0] // (blocks * CHIPS)
    block = rows * CHIPS
    slope = slope_ref[pl.program_id(0)]
    order = order_rows(pos_ref, blocks, rows)
    for nat, held in order:
        qs[nat : nat + rows] = q_ref[pl.ds(held, rows), :]
        ks[nat : nat + rows] = k_ref[pl.ds(held, rows), :]
        vs[nat : nat + rows] = v_ref[pl.ds(held, rows), :]
    for b in range(blocks):
        end = (b + 1) * block
        probs = block_probs(qs[b * block : end], ks[:end], slope, b * block, scale)
        ctx = dot(probs.astype(BF16), vs[:end]).astype(BF16)
        for q in range(CHIPS):
            held = order[b * CHIPS + q][1]
            ctx_ref[pl.ds(held, rows), :] = ctx[q * rows : (q + 1) * rows]


def attend_back_kernel(
    blocks, scale, pos_ref, slope_ref, q_ref, k_ref, v_ref, g_ref, gq_ref, gk_ref, gv_ref,
    qs, ks, vs, gs, gks, gvs,
):
    rows = q_ref.shape[0] // (blocks * CHIPS)
    block = rows * CHIPS
    slope = slope_ref[pl.program_id(0)]
    order = order_rows(pos_ref, blocks, rows)
    for nat, held in order:
        qs[nat : nat + rows] = q_ref[pl.ds(held, rows), :]
        ks[nat : nat + rows] = k_ref[pl.ds(held, rows), :]
        vs[nat : nat + rows] = v_ref[pl.ds(held, rows), :]
        gs[nat : nat + rows] = g_ref[pl.ds(held, rows), :]
    for b in reversed(range(blocks)):
        start, end = b * block, (b + 1) * block
        q, g = qs[start:end], gs[start:end]
        keys, values = ks[:end], vs[:end]
        probs = block_probs(q, keys, slope, start, scale)
        grad_values = dot_tn(probs.astype(BF16), g)
        grad_probs = dot_nt(g, values)
        inner = jnp.sum(probs * grad_probs, axis=-1, keepdims=True)
        grad_scores = (probs * (grad_probs - inner)).astype(BF16)
        grad_q = (dot(grad_scores, keys) * scale).astype(BF16)
        grad_keys = dot_tn(grad_scores, q)
        if b == blocks - 1:
            gks[...] = grad_keys
            gvs[...] = grad_values
        else:
            gks[:end] += grad_keys
            gvs[:end] += grad_values
        for c in range(CHIPS):
            held = order[b * CHIPS + c][1]
            gq_ref[pl.ds(held, rows), :] = grad_q[c * rows : (c + 1) * rows]
    for nat, held in order:
        gk_ref[pl.ds(held, rows), :] = (gks[nat : nat + rows] * scale).astype(BF16)
        gv_ref[pl.ds(held, rows), :] = gvs[nat : nat + rows].astype(BF16)


def attend(qkv, place, slopes):
    length, heads = qkv.shape[0], qkv.shape[1] // (3 * HEAD_DIM)
    blocks = lax.axis_size("z")
    smem = pl.BlockSpec(memory_space=pltpu.SMEM)
    column = lambda first: pl.BlockSpec((length, HEAD_DIM), lambda h: (0, first + h))
    held = pltpu.VMEM((length, HEAD_DIM), BF16)
    return pl.pallas_call(
        partial(attend_kernel, blocks, HEAD_DIM**-0.5),
        grid=(heads,),
        in_specs=[smem, smem, column(0), column(heads), column(2 * heads)],
        out_specs=column(0),
        out_shape=jax.ShapeDtypeStruct((length, heads * HEAD_DIM), BF16),
        scratch_shapes=[held] * 3,
        compiler_params=pltpu.CompilerParams(vmem_limit_bytes=VMEM_LIMIT),
        cost_estimate=pl.CostEstimate(
            flops=6 * length * length * HEAD_DIM * heads,
            bytes_accessed=16 * length * heads * HEAD_DIM,
            transcendentals=2 * length * length * heads,
        ),
    )(place, slopes, qkv, qkv, qkv)


def attend_back(qkv, grad_ctx, place, slopes):
    length, heads = qkv.shape[0], qkv.shape[1] // (3 * HEAD_DIM)
    blocks = lax.axis_size("z")
    smem = pl.BlockSpec(memory_space=pltpu.SMEM)
    column = lambda first: pl.BlockSpec((length, HEAD_DIM), lambda h: (0, first + h))
    held = pltpu.VMEM((length, HEAD_DIM), BF16)
    wide = pltpu.VMEM((length, HEAD_DIM), F32)
    return pl.pallas_call(
        partial(attend_back_kernel, blocks, HEAD_DIM**-0.5),
        grid=(heads,),
        in_specs=[smem, smem, column(0), column(heads), column(2 * heads), column(0)],
        out_specs=[column(0)] * 3,
        out_shape=[jax.ShapeDtypeStruct((length, heads * HEAD_DIM), BF16)] * 3,
        scratch_shapes=[held] * 4 + [wide] * 2,
        compiler_params=pltpu.CompilerParams(vmem_limit_bytes=VMEM_LIMIT),
        cost_estimate=pl.CostEstimate(
            flops=16 * length * length * HEAD_DIM * heads,
            bytes_accessed=28 * length * heads * HEAD_DIM,
            transcendentals=2 * length * length * heads,
        ),
    )(place, slopes, qkv, qkv, qkv, grad_ctx)


def feed_kernel(norm_ref, top_ref, up_ref, down_ref, bias_ref, hidden_ref, grad_ref, term_ref):
    pre = dot(norm_ref[...], up_ref[...]) + bias_ref[...]
    scale = (2.0 / np.pi) ** 0.5
    square = pre * pre
    bend = jnp.tanh(scale * (pre + 0.044715 * (pre * square)))
    cdf = 0.5 + 0.5 * bend
    hidden_ref[...] = (pre * cdf).astype(BF16)
    slope = cdf + (0.5 * scale) * pre * (1.0 - bend * bend) * (1.0 + (3.0 * 0.044715) * square)
    grad = (dot_nt(top_ref[...], down_ref[...]) * slope).astype(BF16)
    grad_ref[...] = grad
    term_ref[...] = dot_nt(grad, up_ref[...]).astype(BF16)


def feed(normed, top, w_up, w_down, bias):
    rows, width = normed.shape
    part = w_up.shape[1]
    tile = min(rows, 256)
    wide = pl.BlockSpec((tile, width), lambda i: (i, 0))
    slim = pl.BlockSpec((tile, part), lambda i: (i, 0))
    whole = lambda v: pl.BlockSpec(v.shape, lambda i: (0, 0))
    bias = bias.reshape(1, part)
    return pl.pallas_call(
        feed_kernel,
        grid=(rows // tile,),
        in_specs=[wide, wide, whole(w_up), whole(w_down), whole(bias)],
        out_specs=[slim, slim, wide],
        out_shape=[
            jax.ShapeDtypeStruct((rows, part), BF16),
            jax.ShapeDtypeStruct((rows, part), BF16),
            jax.ShapeDtypeStruct((rows, width), BF16),
        ],
        compiler_params=pltpu.CompilerParams(vmem_limit_bytes=VMEM_LIMIT),
        cost_estimate=pl.CostEstimate(
            flops=6 * rows * width * part,
            bytes_accessed=6 * rows * width + 4 * rows * part + 4 * width * part,
            transcendentals=rows * part,
        ),
    )(normed, top, w_up, w_down, bias)


def weight_kernel(count, left_0, left_1, *refs):
    rights, out_ref = refs[:-1], refs[-1]
    first = 0
    for i in range(count):
        a, b = rights[2 * i], rights[2 * i + 1]
        cols = a.shape[1]
        out = dot_tn(left_0[...], a[...]) + dot_tn(left_1[...], b[...])
        out_ref[..., first : first + cols] = out.astype(BF16).reshape(out_ref.shape[:-1] + (cols,))
        first += cols


def weight_grad(left, rights, owner_rows=None):
    rows, width = left[0].shape
    cols = sum(r[0].shape[1] for r in rights)
    if owner_rows and lax.axis_size("o") > 1:
        joined = [jnp.concatenate(v, axis=1) for v in zip(*rights)]
        grad = (dot_tn(left[0], joined[0]) + dot_tn(left[1], joined[1])).astype(BF16)
        return by_owner(grad, owner_rows)
    tile = 256
    if owner_rows:
        z_size = lax.axis_size("z")
        tile = z_size * owner_rows
        shape = (z_size, width // tile, owner_rows, cols)
        out_spec = pl.BlockSpec((z_size, 1, owner_rows, cols), lambda i: (0, i, 0, 0))
    else:
        shape = (width, cols)
        out_spec = pl.BlockSpec((tile, cols), lambda i: (i, 0))
    flat = [v for r in rights for v in r]
    out = pl.pallas_call(
        partial(weight_kernel, len(rights)),
        grid=(width // tile,),
        in_specs=[pl.BlockSpec((rows, tile), lambda i: (0, i))] * 2
        + [pl.BlockSpec(v.shape, lambda i: (0, 0)) for v in flat],
        out_specs=out_spec,
        out_shape=jax.ShapeDtypeStruct(shape, BF16),
        compiler_params=pltpu.CompilerParams(vmem_limit_bytes=VMEM_LIMIT),
        cost_estimate=pl.CostEstimate(
            flops=4 * rows * width * cols,
            bytes_accessed=4 * rows * (width + cols) + 2 * width * cols,
            transcendentals=0,
        ),
    )(*left, *flat)
    return out.reshape(width, cols)


def terms_kernel(*refs):
    weight_ref, out_ref = refs[-2:]
    total, first = 0.0, 0
    for ref in refs[:-2]:
        total = total + dot_nt(ref[...], weight_ref[:, first : first + ref.shape[1]])
        first += ref.shape[1]
    out_ref[...] = total.astype(BF16)


def terms(lefts, weight):
    rows, width = lefts[0].shape[0], weight.shape[0]
    tile = min(rows, 256)
    return pl.pallas_call(
        terms_kernel,
        grid=(rows // tile,),
        in_specs=[pl.BlockSpec((tile, v.shape[1]), lambda i: (i, 0)) for v in lefts]
        + [pl.BlockSpec(weight.shape, lambda i: (0, 0))],
        out_specs=pl.BlockSpec((tile, width), lambda i: (i, 0)),
        out_shape=jax.ShapeDtypeStruct((rows, width), BF16),
        compiler_params=pltpu.CompilerParams(vmem_limit_bytes=VMEM_LIMIT),
        cost_estimate=pl.CostEstimate(
            flops=2 * rows * weight.size,
            bytes_accessed=2 * weight.size + 4 * rows * width,
            transcendentals=0,
        ),
    )(*lefts, weight)


def norm_forward(values, gain, shift):
    centre = values - jnp.mean(values, axis=-1, keepdims=True)
    factor = lax.rsqrt(jnp.mean(centre * centre, axis=-1, keepdims=True) + EPS_NORM)
    normed = centre * factor
    return (normed * gain + shift, normed, factor)


def norm_backward(incoming, normed, factor, gain):
    scaled = incoming * gain
    input_grad = factor * (
        scaled
        - jnp.mean(scaled, axis=-1, keepdims=True)
        - normed * jnp.mean(scaled * normed, axis=-1, keepdims=True)
    )
    return (input_grad, jnp.sum(incoming * normed, axis=0), jnp.sum(incoming, axis=0))


def adam_step(weight, first, second, grad, scalars):
    clip, keep_first, keep_second, fix_first, fix_second, rate, decay = scalars
    scaled = grad * clip
    first = keep_first * first + (1.0 - keep_first) * scaled
    second = keep_second * second + (1.0 - keep_second) * scaled * scaled
    change = -rate * (
        first * fix_first / (jnp.sqrt(second * fix_second) + EPS_ADAM) + decay * weight
    )
    return first, second, change


def adam_kernel(as_step, scalar_ref, weight_ref, moment_ref, grad_ref, out_ref, new_ref):
    scalars = [scalar_ref[i] for i in range(7)]
    weight = weight_ref[...].astype(F32)
    grad = grad_ref[...].reshape(weight.shape).astype(F32)
    first, second, change = adam_step(weight, moment_ref[0], moment_ref[1], grad, scalars)
    new_ref[0] = first
    new_ref[1] = second
    out_ref[...] = change if as_step else (weight + change).astype(BF16)


def adam_update(weight, moments, grad, scalars, as_step=False):
    rows, cols = weight.shape
    if grad.ndim == 2:
        high, wide = (16 if cols > 4096 else max(16, rows // 4)), cols
        grid, where, grad_block, grad_where = (rows // high,), (lambda i: (i, 0)), (high, wide), (lambda i: (i, 0))
    else:
        high, wide = rows, grad.shape[2]
        grid, where, grad_block, grad_where = (GROUP,), (lambda i: (0, i)), (1, rows, wide), (lambda i: (i, 0, 0))
    tile = pl.BlockSpec((high, wide), where)
    pair = pl.BlockSpec((2, high, wide), lambda i: (0,) + where(i))
    return pl.pallas_call(
        partial(adam_kernel, as_step),
        grid=grid,
        in_specs=[
            pl.BlockSpec(memory_space=pltpu.SMEM),
            tile,
            pair,
            pl.BlockSpec(grad_block, grad_where),
        ],
        out_specs=[tile, pair],
        out_shape=[
            jax.ShapeDtypeStruct(weight.shape, F32 if as_step else BF16),
            jax.ShapeDtypeStruct(moments.shape, F32),
        ],
        compiler_params=pltpu.CompilerParams(vmem_limit_bytes=VMEM_LIMIT),
        cost_estimate=pl.CostEstimate(
            flops=20 * weight.size, bytes_accessed=22 * weight.size, transcendentals=weight.size
        ),
    )(scalars, weight, moments, grad)


def column_sum(values):
    return jnp.sum(values.astype(F32), axis=0)


def body(
    tokens,
    cotangent,
    qkv_weight,
    out_weight,
    up_weight,
    down_weight,
    vectors,
    qkv_moments,
    out_moments,
    up_moments,
    down_moments,
    vector_moments,
    step,
    hyper,
):
    chip = lax.axis_index("chip")
    p = lax.axis_index(PLANE)
    devices = lax.axis_size(AXES)
    width = tokens.shape[2]
    place = jnp.stack([chip, lax.axis_index("z")]).astype(jnp.int32)
    heads = HEADS // GROUP
    head_ids = (p * heads + jnp.arange(heads)).astype(F32)
    slopes = jnp.exp2(-8.0 * (head_ids + 1.0) / HEADS)
    tokens_given, top_given = tokens[0], cotangent[0]

    flat = lax.axis_index(AXES)
    vecs = lax.dynamic_update_slice(
        jnp.zeros((vectors.shape[0], width), BF16), vectors, (0, flat * vectors.shape[1])
    )
    vecs = sum_all(vecs).astype(F32)
    qkv_parts = trade_columns(qkv_weight, 3)
    pair_qkv = pair_up(qkv_parts, out_weight, True)
    tokens_given, pair_qkv = together(tokens_given, pair_qkv)
    rows_low = trade(trade(tokens_given, "chip"), "z")
    rows_low, pair_qkv = together(rows_low, pair_qkv)
    full_qkv, full_out = gather_pair(pair_qkv, qkv_parts, out_weight, p, True)
    top_given, up_weight, rows_low = together(top_given, up_weight, rows_low)
    held_top = trade(top_given, "chip")
    up_parts = trade_columns(up_weight, 1)
    rows_low, up_parts, held_top = together(rows_low, up_parts, held_top)
    rows_in = in_z_order(rows_low).astype(F32)
    normed, hat_one, factor_one = norm_forward(rows_in, vecs[0], vecs[1])
    normed_low, held_top = together(normed.astype(BF16), held_top)
    own = plane_order(normed_low)
    top_low = trade(held_top, "z")
    own, top_low, up_parts, w_qkv, w_out = together(own, top_low, up_parts, full_qkv, full_out)
    top_low = in_z_order(top_low)
    full_up = lax.all_gather(up_parts, ("o", "z"), axis=0, tiled=True)
    full_down = gather_rows(down_weight, p)
    own = jnp.concatenate(own, axis=0)
    own, top_low = together(own, top_low)
    normed_a = [own, swap_cores(own)]
    top_own = plane_order(top_low)
    part = width // GROUP
    bias_q = lax.dynamic_slice(vecs[2], (p * part,), (part,))
    bias_v = lax.dynamic_slice(vecs[3], (p * part,), (part,))
    bias_qkv = jnp.concatenate([bias_q, jnp.zeros_like(bias_q), bias_v])
    qkv = [(dot(v, w_qkv) + bias_qkv).astype(BF16) for v in normed_a]
    context = [attend(v, place, slopes) for v in qkv]
    context, top_own = together(context, top_own)
    top_own = jnp.concatenate(top_own, axis=0)
    term_other = dot(context[1], w_out).astype(BF16)
    term_own = dot(after(context[0], term_other), w_out).astype(BF16)
    pieces = chip_exchange(core_pieces(term_own, term_other))
    pieces, top_own, full_up = together(pieces, top_own, full_up)
    w_up = in_row_order(full_up, up_parts.shape[2])
    residual = rows_in + add_up(pieces) + vecs[4]
    normed, hat_two, factor_two = norm_forward(residual, vecs[5], vecs[6])
    normed_low = normed.astype(BF16)
    own = plane_order(normed_low)
    grad_mlp = [top_own, swap_cores(top_own)]
    own, grad_mlp, w_down, w_up = together(own, grad_mlp, full_down, w_up)
    own = jnp.concatenate(own, axis=0)
    normed_b = [own, swap_cores(own)]
    hidden_part = w_up.shape[1]
    bias_up = lax.dynamic_slice(vecs[8:].reshape(-1), (p * hidden_part,), (hidden_part,))

    hidden_other, grad_other, term_other = feed(normed_b[1], grad_mlp[1], w_up, w_down, bias_up)
    left, term_other = together(normed_b[0], term_other)
    hidden_own, grad_own, term_own = feed(left, grad_mlp[0], w_up, w_down, bias_up)
    hidden, grad_pre = [hidden_own, hidden_other], [grad_own, grad_other]
    pieces, held = together(core_pieces(term_own, term_other), hidden)
    grad_down = weight_grad(held, [grad_mlp])
    owned_down = scatter_rows(grad_down, p)
    pieces = chip_exchange(pieces)
    held, grad_down = together(grad_pre, grad_down)
    grad_up = weight_grad(normed_b, [held], up_weight.shape[0])
    pieces, grad_up = together(pieces, grad_up)
    grad_normed = add_up(pieces)
    through, gain_two_grad, shift_two_grad = norm_backward(grad_normed, hat_two, factor_two, vecs[5])
    grad_residual = top_low.astype(F32) + through
    grad_attn_own = grad_residual.astype(BF16)

    own = plane_order(grad_attn_own)
    held, grad_attn_own = together(hidden, grad_attn_own)
    mlp_other = dot(held[1], w_down).astype(BF16)
    mlp_own = dot(after(held[0], mlp_other), w_down).astype(BF16)
    reduced_up = scatter_columns(grad_up)
    mlp_sums = core_pieces(mlp_own, mlp_other)
    own, mlp_sums, owned_down = together(own, mlp_sums, owned_down)
    own = jnp.concatenate(own, axis=0)
    own, mlp_sums = together(own, mlp_sums)
    grad_attn = [own, swap_cores(own)]

    mlp_parts = chip_trade(mlp_sums, chip)
    grad_context = [dot_nt(v, w_out).astype(BF16) for v in grad_attn]
    grads = [attend_back(v, g, place, slopes) for v, g in zip(qkv, grad_context)]
    grads, reduced_up = together(grads, reduced_up)
    grad_qkv_weight = weight_grad(normed_a, list(zip(*grads)), qkv_weight.shape[0])
    held, grad_attn, grad_qkv_weight = together(context, grad_attn, grad_qkv_weight)
    grad_out = (dot_tn(held[0], grad_attn[0]) + dot_tn(held[1], grad_attn[1])).astype(BF16)
    grads, grad_out, mlp_parts = together(grads, grad_out, mlp_parts)
    term_other = terms(grads[1], w_qkv)
    owned_up = trade_rows(reduced_up)
    held, term_other, owned_up = together(grads[0], term_other, owned_up)
    term_own = terms(held, w_qkv)
    pieces = core_pieces(term_own, term_other)
    reduced_qkv, owned_out = scatter_pair(
        grad_qkv_weight, grad_out, qkv_weight.shape[0], p
    )
    pieces = chip_exchange(pieces)
    grad_normed = add_up(pieces)
    through, gain_one_grad, shift_one_grad = norm_backward(grad_normed, hat_one, factor_one, vecs[0])
    result = (residual + sum_parts(mlp_parts) + vecs[7]).astype(BF16)
    result, reduced_qkv = together(result, reduced_qkv)
    owned_qkv = trade_rows(reduced_qkv)
    bias_grads = [column_sum(grads[0][i]) + column_sum(grads[1][i]) for i in (0, 2)]
    up_bias_grad = column_sum(grad_own) + column_sum(grad_other)
    wide = lambda v: lax.dynamic_update_slice(jnp.zeros((width,), F32), v, (p * part,))
    up_wide = lax.dynamic_update_slice(
        jnp.zeros((GROUP * hidden_part,), F32), up_bias_grad, (p * hidden_part,)
    )
    vector_grad = jnp.concatenate(
        [
            jnp.stack(
                [
                    gain_one_grad,
                    shift_one_grad,
                    wide(bias_grads[0]),
                    wide(bias_grads[1]),
                    column_sum(grad_attn_own),
                    gain_two_grad,
                    shift_two_grad,
                    column_sum(top_given),
                ]
            ),
            up_wide.reshape(-1, width),
        ],
        axis=0,
    )
    vec_parts = vector_grad.reshape(vectors.shape[0], devices, -1).transpose(1, 0, 2)
    owned_vec = jnp.sum(trade(vec_parts, AXES), axis=0)

    grad_qkv_rows = owned_qkv.reshape(GROUP, -1, 3, part).transpose(1, 2, 0, 3).reshape(qkv_weight.shape)
    squares = [jnp.sum(jnp.square(g.astype(F32))) for g in (owned_qkv, owned_out, owned_up, owned_down, owned_vec)]
    squares = jnp.broadcast_to(sum(squares), (devices, 1))
    grad_norm = jnp.sqrt(jnp.sum(trade(squares, AXES)))
    back = (grad_residual + through).astype(BF16)
    result, back = from_planes(result), from_planes(back)
    result, back, grad_norm = together(result, back, grad_norm)
    both = to_owners([jnp.concatenate(v, axis=1) for v in zip(result, back)])
    clip_factor = jnp.minimum(1.0, hyper[4] / (grad_norm + 1e-06))
    step_float = step.astype(F32)
    fix_first = 1.0 / (1.0 - hyper[2] ** step_float)
    fix_second = 1.0 / (1.0 - hyper[3] ** step_float)
    scalars = [clip_factor, hyper[2], hyper[3], fix_first, fix_second, hyper[0], hyper[1]]
    listed = jnp.stack(scalars)
    new_qkv, new_qkv_moments = adam_update(qkv_weight, qkv_moments, grad_qkv_rows, listed)
    out_step, new_out_moments = adam_update(out_weight, out_moments, owned_out, listed, as_step=True)
    new_up, new_up_moments = adam_update(up_weight, up_moments, owned_up, listed)
    new_down, new_down_moments = adam_update(down_weight, down_moments, owned_down, listed)
    both, new_qkv, out_step, new_up, new_down = together(both, new_qkv, out_step, new_up, new_down)
    activations, input_grad = both[:, :width], both[:, width:]
    first, second, vector_step = adam_step(
        vectors.astype(F32), vector_moments[0], vector_moments[1], owned_vec, scalars
    )
    return (
        activations[None],
        input_grad[None],
        grad_norm,
        new_qkv,
        out_step,
        new_up,
        new_down,
        vector_step,
        new_qkv_moments,
        new_out_moments,
        new_up_moments,
        new_down_moments,
        jnp.stack([first, second]),
    )


def solution(mesh):
    devices = np.asarray(mesh.devices)
    planes = Mesh(devices.reshape(-1, CHIPS, 2, devices.shape[1]), AXES)
    rows = P(AXES, None)
    seqs = P(("o",) + PLANE, "z", None)
    pair = P(None, AXES, None)
    cols = P(None, AXES)
    return jax.shard_map(
        body,
        mesh=planes,
        in_specs=(seqs, seqs, rows, rows, rows, rows, cols)
        + (pair, pair, pair, pair, P(None, None, AXES), P(), P()),
        out_specs=(seqs, seqs, P(), rows, rows, rows, rows, cols)
        + (pair, pair, pair, pair, P(None, None, AXES)),
        check_vma=False,
    )
```

```python
from functools import partial

import jax
import jax.numpy as jnp
import numpy as np
from jax import lax
from jax.experimental import pallas as pl
from jax.experimental.pallas import tpu as pltpu
from jax.sharding import Mesh
from jax.sharding import PartitionSpec as P

HEADS = 16
HEAD_DIM = 128
GROUP = 8
CHIPS = GROUP // 2

EPS_NORM = 1e-05
EPS_ADAM = 1e-08
F32 = jnp.float32
BF16 = jnp.bfloat16
PLANE = ("chip", "core")
AXES = ("o",) + PLANE + ("z",)
VMEM_LIMIT = 56 * 1024 * 1024


def after(value, *others):
    return lax.optimization_barrier((value,) + others)[0]


def together(*values):
    return lax.optimization_barrier(values)


def dot(a, b):
    return jnp.dot(a, b, preferred_element_type=F32)


def dot_nt(a, b):
    return lax.dot_general(a, b, (((1,), (1,)), ((), ())), preferred_element_type=F32)


def dot_tn(a, b):
    return lax.dot_general(a, b, (((0,), (0,)), ((), ())), preferred_element_type=F32)


def swap_chips(value, k):
    return lax.ppermute(value, "chip", [(q, q ^ k) for q in range(CHIPS)])


def swap_cores(value):
    return lax.ppermute(value, "core", [(0, 1), (1, 0)])


def swap(value, axis, k):
    return lax.ppermute(value, axis, [(i, i ^ k) for i in range(lax.axis_size(axis))])


def sum_all(value):
    for axis in AXES:
        k = 1
        while k < lax.axis_size(axis):
            value = value + swap(value, axis, k)
            k *= 2
    return value


def trade(value, axes):
    return lax.all_to_all(value, axes, 0, 0, tiled=True)


def pick(stacked, index):
    return lax.dynamic_index_in_dim(stacked, index, 0, keepdims=False)


def plane_order(own):
    return [own] + [swap_chips(own, k) for k in range(1, CHIPS)]


def to_planes(parts):
    z = lax.axis_index("z")
    return [pick(parts, z)] + [swap(pick(parts, z ^ k), "z", k) for k in range(1, CHIPS)]


def in_z_order(natural):
    z = lax.axis_index("z")
    parts = natural.reshape(CHIPS, -1, natural.shape[1])
    return jnp.concatenate([pick(parts, z ^ k) for k in range(CHIPS)], axis=0)


def from_planes(block):
    parts = block.reshape(CHIPS, -1, block.shape[1])
    return [parts[0]] + [swap(parts[k], "z", k) for k in range(1, CHIPS)]


def by_chip(pieces):
    z = lax.axis_index("z")
    held = jnp.stack(pieces)
    return jnp.concatenate([pick(held, z ^ q) for q in range(CHIPS)], axis=0)


def core_pieces(own_terms, other_terms):
    rows = own_terms.shape[0] // CHIPS
    arrived = swap_cores(other_terms)
    near = own_terms[:rows].astype(F32) + arrived[:rows].astype(F32)
    far = (own_terms[rows:].astype(F32) + arrived[rows:].astype(F32)).astype(BF16)
    return [near] + [far[k * rows : (k + 1) * rows] for k in range(CHIPS - 1)]


def chip_exchange(pieces):
    return pieces[:1] + [swap_chips(v, k) for k, v in enumerate(pieces) if k]


def add_up(pieces):
    return sum(v.astype(F32) for v in pieces)


def sum_parts(parts):
    return jnp.sum(parts.reshape(CHIPS, -1, parts.shape[1]).astype(F32), axis=0)


def chip_trade(pieces, chip):
    parts = jnp.stack([pieces[0].astype(BF16)] + pieces[1:])
    low = jnp.concatenate([pick(parts, chip ^ q) for q in range(CHIPS)], axis=0)
    return trade(low, "chip")


def trade_columns(weight, groups):
    rows, cols = weight.shape
    width = cols // (groups * GROUP)
    parts = weight.reshape(rows, groups, GROUP, width).transpose(2, 0, 1, 3)
    parts = parts.reshape(GROUP, rows, groups * width)
    return trade(parts, PLANE)


def side_by_side(stack, count):
    rows = stack.shape[0] // count
    return stack.reshape(count, rows, -1).transpose(1, 0, 2).reshape(rows, -1)


def stacked(wide, count):
    rows = wide.shape[0]
    return wide.reshape(rows, count, -1).transpose(1, 0, 2).reshape(count * rows, -1)


def in_row_order(full, width):
    o_size, z_size = lax.axis_size("o"), lax.axis_size("z")
    full = full.reshape(o_size, z_size, GROUP, -1, width).transpose(0, 2, 1, 3, 4)
    return full.reshape(-1, width)


def pair_up(parts, rows_weight, beside):
    width = parts.shape[2]
    flat = parts.reshape(-1, width)
    if lax.axis_size("o") > 1:
        return (flat, rows_weight)
    count = GROUP if beside else rows_weight.shape[1] // width
    return (jnp.concatenate([flat, after(stacked(rows_weight, count), ())], axis=1 if beside else 0),)


def gather_pair(pair, parts, rows_weight, p, beside):
    width = parts.shape[2]
    if len(pair) > 1:
        full = lax.all_gather(pair[0], ("o", "z"), axis=0, tiled=True)
        others = lax.all_gather(pair[1], AXES, axis=0, tiled=True)
        return in_row_order(full, width), pick(others.reshape(GROUP, -1, rows_weight.shape[1]), p)
    full = lax.all_gather(pair[0], "z", axis=0, tiled=False)
    first, second = jnp.split(full, [width if beside else parts.size // width], axis=2 if beside else 1)
    count = GROUP if beside else rows_weight.shape[1] // width
    second = [side_by_side(second[i], count) for i in range(full.shape[0])]
    return in_row_order(first, width), jnp.concatenate(second, axis=0)


def scatter_pair(grad_columns, grad_rows, rows, p):
    width = grad_columns.shape[1]
    if lax.axis_size("o") > 1:
        return scatter_columns(grad_columns), scatter_rows(grad_rows, p)
    z_size = lax.axis_size("z")
    beside = grad_rows.reshape(z_size, -1, grad_rows.shape[1])
    beside = after(jnp.concatenate([stacked(beside[i], GROUP) for i in range(z_size)], axis=0), ())
    both = jnp.concatenate([grad_columns, beside], axis=1)
    mine = lax.psum_scatter(both, "z", scatter_dimension=0, tiled=True)
    return mine[:, :width].reshape(GROUP, rows, width), side_by_side(mine[:, width:], GROUP)


def by_owner(grad, rows):
    o_size, z_size = lax.axis_size("o"), lax.axis_size("z")
    parts = grad.reshape(o_size, GROUP, z_size, rows, -1).transpose(0, 2, 1, 3, 4)
    return parts.reshape(grad.shape)


def scatter_columns(parts):
    mine = lax.psum_scatter(parts, ("o", "z"), scatter_dimension=0, tiled=True)
    return mine.reshape(GROUP, -1, parts.shape[1])


def trade_rows(parts):
    return trade(parts, PLANE)


def gather_rows(weight, p):
    if lax.axis_size("o") == 1:
        return lax.all_gather(weight, "z", axis=0, tiled=True)
    full = lax.all_gather(weight, AXES, axis=0, tiled=True)
    return pick(full.reshape(GROUP, -1, weight.shape[1]), p)


def scatter_rows(grad, p):
    if lax.axis_size("o") == 1:
        return lax.psum_scatter(grad, "z", scatter_dimension=0, tiled=True)
    full = jnp.zeros((GROUP,) + grad.shape, grad.dtype)
    full = lax.dynamic_update_index_in_dim(full, grad, p, 0)
    full = full.reshape(-1, grad.shape[1])
    return lax.psum_scatter(full, AXES, scatter_dimension=0, tiled=True)


def order_rows(pos_ref, blocks, rows):
    out = []
    for b in range(blocks):
        for q in range(CHIPS):
            held = ((q ^ pos_ref[0]) * blocks + (b ^ pos_ref[1])) * rows
            out.append(((b * CHIPS + q) * rows, pl.multiple_of(held, rows)))
    return out


def block_probs(q, keys, slope, start, scale):
    scores = dot_nt(q, keys) * scale
    row = lax.broadcasted_iota(jnp.int32, scores.shape, 0) + start
    col = lax.broadcasted_iota(jnp.int32, scores.shape, 1)
    scores = scores - slope * jnp.abs(row - col).astype(F32)
    expo = jnp.exp(scores - jnp.max(scores, axis=-1, keepdims=True))
    return expo * (1.0 / jnp.sum(expo, axis=-1, keepdims=True))


def attend_kernel(blocks, scale, pos_ref, slope_ref, q_ref, k_ref, v_ref, ctx_ref, qs, ks, vs):
    rows = q_ref.shape[0] // (blocks * CHIPS)
    block = rows * CHIPS
    slope = slope_ref[pl.program_id(0)]
    order = order_rows(pos_ref, blocks, rows)
    for nat, held in order:
        qs[nat : nat + rows] = q_ref[pl.ds(held, rows), :]
        ks[nat : nat + rows] = k_ref[pl.ds(held, rows), :]
        vs[nat : nat + rows] = v_ref[pl.ds(held, rows), :]
    for b in range(blocks):
        end = (b + 1) * block
        probs = block_probs(qs[b * block : end], ks[:end], slope, b * block, scale)
        ctx = dot(probs.astype(BF16), vs[:end]).astype(BF16)
        for q in range(CHIPS):
            held = order[b * CHIPS + q][1]
            ctx_ref[pl.ds(held, rows), :] = ctx[q * rows : (q + 1) * rows]


def attend_back_kernel(
    blocks, scale, pos_ref, slope_ref, q_ref, k_ref, v_ref, g_ref, gq_ref, gk_ref, gv_ref,
    qs, ks, vs, gs, gks, gvs,
):
    rows = q_ref.shape[0] // (blocks * CHIPS)
    block = rows * CHIPS
    slope = slope_ref[pl.program_id(0)]
    order = order_rows(pos_ref, blocks, rows)
    for nat, held in order:
        qs[nat : nat + rows] = q_ref[pl.ds(held, rows), :]
        ks[nat : nat + rows] = k_ref[pl.ds(held, rows), :]
        vs[nat : nat + rows] = v_ref[pl.ds(held, rows), :]
        gs[nat : nat + rows] = g_ref[pl.ds(held, rows), :]
    for b in reversed(range(blocks)):
        start, end = b * block, (b + 1) * block
        q, g = qs[start:end], gs[start:end]
        keys, values = ks[:end], vs[:end]
        probs = block_probs(q, keys, slope, start, scale)
        grad_values = dot_tn(probs.astype(BF16), g)
        grad_probs = dot_nt(g, values)
        inner = jnp.sum(probs * grad_probs, axis=-1, keepdims=True)
        grad_scores = (probs * (grad_probs - inner)).astype(BF16)
        grad_q = (dot(grad_scores, keys) * scale).astype(BF16)
        grad_keys = dot_tn(grad_scores, q)
        if b == blocks - 1:
            gks[...] = grad_keys
            gvs[...] = grad_values
        else:
            gks[:end] += grad_keys
            gvs[:end] += grad_values
        for c in range(CHIPS):
            held = order[b * CHIPS + c][1]
            gq_ref[pl.ds(held, rows), :] = grad_q[c * rows : (c + 1) * rows]
    for nat, held in order:
        gk_ref[pl.ds(held, rows), :] = (gks[nat : nat + rows] * scale).astype(BF16)
        gv_ref[pl.ds(held, rows), :] = gvs[nat : nat + rows].astype(BF16)


def attend(qkv, place, slopes):
    length, heads = qkv.shape[0], qkv.shape[1] // (3 * HEAD_DIM)
    blocks = lax.axis_size("z")
    smem = pl.BlockSpec(memory_space=pltpu.SMEM)
    column = lambda first: pl.BlockSpec((length, HEAD_DIM), lambda h: (0, first + h))
    held = pltpu.VMEM((length, HEAD_DIM), BF16)
    return pl.pallas_call(
        partial(attend_kernel, blocks, HEAD_DIM**-0.5),
        grid=(heads,),
        in_specs=[smem, smem, column(0), column(heads), column(2 * heads)],
        out_specs=column(0),
        out_shape=jax.ShapeDtypeStruct((length, heads * HEAD_DIM), BF16),
        scratch_shapes=[held] * 3,
        compiler_params=pltpu.CompilerParams(vmem_limit_bytes=VMEM_LIMIT),
        cost_estimate=pl.CostEstimate(
            flops=6 * length * length * HEAD_DIM * heads,
            bytes_accessed=16 * length * heads * HEAD_DIM,
            transcendentals=2 * length * length * heads,
        ),
    )(place, slopes, qkv, qkv, qkv)


def attend_back(qkv, grad_ctx, place, slopes):
    length, heads = qkv.shape[0], qkv.shape[1] // (3 * HEAD_DIM)
    blocks = lax.axis_size("z")
    smem = pl.BlockSpec(memory_space=pltpu.SMEM)
    column = lambda first: pl.BlockSpec((length, HEAD_DIM), lambda h: (0, first + h))
    held = pltpu.VMEM((length, HEAD_DIM), BF16)
    wide = pltpu.VMEM((length, HEAD_DIM), F32)
    return pl.pallas_call(
        partial(attend_back_kernel, blocks, HEAD_DIM**-0.5),
        grid=(heads,),
        in_specs=[smem, smem, column(0), column(heads), column(2 * heads), column(0)],
        out_specs=[column(0)] * 3,
        out_shape=[jax.ShapeDtypeStruct((length, heads * HEAD_DIM), BF16)] * 3,
        scratch_shapes=[held] * 4 + [wide] * 2,
        compiler_params=pltpu.CompilerParams(vmem_limit_bytes=VMEM_LIMIT),
        cost_estimate=pl.CostEstimate(
            flops=16 * length * length * HEAD_DIM * heads,
            bytes_accessed=28 * length * heads * HEAD_DIM,
            transcendentals=2 * length * length * heads,
        ),
    )(place, slopes, qkv, qkv, qkv, grad_ctx)


def feed_kernel(norm_ref, top_ref, up_ref, down_ref, bias_ref, hidden_ref, grad_ref, term_ref):
    pre = dot(norm_ref[...], up_ref[...]) + bias_ref[...]
    scale = (2.0 / np.pi) ** 0.5
    square = pre * pre
    bend = jnp.tanh(scale * (pre + 0.044715 * (pre * square)))
    cdf = 0.5 + 0.5 * bend
    hidden_ref[...] = (pre * cdf).astype(BF16)
    slope = cdf + (0.5 * scale) * pre * (1.0 - bend * bend) * (1.0 + (3.0 * 0.044715) * square)
    grad = (dot_nt(top_ref[...], down_ref[...]) * slope).astype(BF16)
    grad_ref[...] = grad
    term_ref[...] = dot_nt(grad, up_ref[...]).astype(BF16)


def feed(normed, top, w_up, w_down, bias):
    rows, width = normed.shape
    part = w_up.shape[1]
    tile = min(rows, 256)
    wide = pl.BlockSpec((tile, width), lambda i: (i, 0))
    slim = pl.BlockSpec((tile, part), lambda i: (i, 0))
    whole = lambda v: pl.BlockSpec(v.shape, lambda i: (0, 0))
    bias = bias.reshape(1, part)
    return pl.pallas_call(
        feed_kernel,
        grid=(rows // tile,),
        in_specs=[wide, wide, whole(w_up), whole(w_down), whole(bias)],
        out_specs=[slim, slim, wide],
        out_shape=[
            jax.ShapeDtypeStruct((rows, part), BF16),
            jax.ShapeDtypeStruct((rows, part), BF16),
            jax.ShapeDtypeStruct((rows, width), BF16),
        ],
        compiler_params=pltpu.CompilerParams(vmem_limit_bytes=VMEM_LIMIT),
        cost_estimate=pl.CostEstimate(
            flops=6 * rows * width * part,
            bytes_accessed=6 * rows * width + 4 * rows * part + 4 * width * part,
            transcendentals=rows * part,
        ),
    )(normed, top, w_up, w_down, bias)


def weight_kernel(count, left_0, left_1, *refs):
    rights, out_ref = refs[:-1], refs[-1]
    first = 0
    for i in range(count):
        a, b = rights[2 * i], rights[2 * i + 1]
        cols = a.shape[1]
        out = dot_tn(left_0[...], a[...]) + dot_tn(left_1[...], b[...])
        out_ref[..., first : first + cols] = out.astype(BF16).reshape(out_ref.shape[:-1] + (cols,))
        first += cols


def weight_grad(left, rights, owner_rows=None):
    rows, width = left[0].shape
    cols = sum(r[0].shape[1] for r in rights)
    if owner_rows and lax.axis_size("o") > 1:
        joined = [jnp.concatenate(v, axis=1) for v in zip(*rights)]
        grad = (dot_tn(left[0], joined[0]) + dot_tn(left[1], joined[1])).astype(BF16)
        return by_owner(grad, owner_rows)
    tile = 256
    if owner_rows:
        z_size = lax.axis_size("z")
        tile = z_size * owner_rows
        shape = (z_size, width // tile, owner_rows, cols)
        out_spec = pl.BlockSpec((z_size, 1, owner_rows, cols), lambda i: (0, i, 0, 0))
    else:
        shape = (width, cols)
        out_spec = pl.BlockSpec((tile, cols), lambda i: (i, 0))
    flat = [v for r in rights for v in r]
    out = pl.pallas_call(
        partial(weight_kernel, len(rights)),
        grid=(width // tile,),
        in_specs=[pl.BlockSpec((rows, tile), lambda i: (0, i))] * 2
        + [pl.BlockSpec(v.shape, lambda i: (0, 0)) for v in flat],
        out_specs=out_spec,
        out_shape=jax.ShapeDtypeStruct(shape, BF16),
        compiler_params=pltpu.CompilerParams(vmem_limit_bytes=VMEM_LIMIT),
        cost_estimate=pl.CostEstimate(
            flops=4 * rows * width * cols,
            bytes_accessed=4 * rows * (width + cols) + 2 * width * cols,
            transcendentals=0,
        ),
    )(*left, *flat)
    return out.reshape(width, cols)


def terms_kernel(*refs):
    weight_ref, out_ref = refs[-2:]
    total, first = 0.0, 0
    for ref in refs[:-2]:
        total = total + dot_nt(ref[...], weight_ref[:, first : first + ref.shape[1]])
        first += ref.shape[1]
    out_ref[...] = total.astype(BF16)


def terms(lefts, weight):
    rows, width = lefts[0].shape[0], weight.shape[0]
    tile = min(rows, 256)
    return pl.pallas_call(
        terms_kernel,
        grid=(rows // tile,),
        in_specs=[pl.BlockSpec((tile, v.shape[1]), lambda i: (i, 0)) for v in lefts]
        + [pl.BlockSpec(weight.shape, lambda i: (0, 0))],
        out_specs=pl.BlockSpec((tile, width), lambda i: (i, 0)),
        out_shape=jax.ShapeDtypeStruct((rows, width), BF16),
        compiler_params=pltpu.CompilerParams(vmem_limit_bytes=VMEM_LIMIT),
        cost_estimate=pl.CostEstimate(
            flops=2 * rows * weight.size,
            bytes_accessed=2 * weight.size + 4 * rows * width,
            transcendentals=0,
        ),
    )(*lefts, weight)


def norm_forward(values, gain, shift):
    centre = values - jnp.mean(values, axis=-1, keepdims=True)
    factor = lax.rsqrt(jnp.mean(centre * centre, axis=-1, keepdims=True) + EPS_NORM)
    normed = centre * factor
    return (normed * gain + shift, normed, factor)


def norm_backward(incoming, normed, factor, gain):
    scaled = incoming * gain
    input_grad = factor * (
        scaled
        - jnp.mean(scaled, axis=-1, keepdims=True)
        - normed * jnp.mean(scaled * normed, axis=-1, keepdims=True)
    )
    return (input_grad, jnp.sum(incoming * normed, axis=0), jnp.sum(incoming, axis=0))


def adam_step(weight, first, second, grad, scalars):
    clip, keep_first, keep_second, fix_first, fix_second, rate, decay = scalars
    scaled = grad * clip
    first = keep_first * first + (1.0 - keep_first) * scaled
    second = keep_second * second + (1.0 - keep_second) * scaled * scaled
    change = -rate * (
        first * fix_first / (jnp.sqrt(second * fix_second) + EPS_ADAM) + decay * weight
    )
    return first, second, change


def adam_kernel(as_step, scalar_ref, weight_ref, moment_ref, grad_ref, out_ref, new_ref):
    scalars = [scalar_ref[i] for i in range(7)]
    weight = weight_ref[...].astype(F32)
    grad = grad_ref[...].reshape(weight.shape).astype(F32)
    first, second, change = adam_step(weight, moment_ref[0], moment_ref[1], grad, scalars)
    new_ref[0] = first
    new_ref[1] = second
    out_ref[...] = change if as_step else (weight + change).astype(BF16)


def adam_update(weight, moments, grad, scalars, as_step=False):
    rows, cols = weight.shape
    if grad.ndim == 2:
        high, wide = (16 if cols > 4096 else max(16, rows // 4)), cols
        grid, where, grad_block, grad_where = (rows // high,), (lambda i: (i, 0)), (high, wide), (lambda i: (i, 0))
    else:
        high, wide = rows, grad.shape[2]
        grid, where, grad_block, grad_where = (GROUP,), (lambda i: (0, i)), (1, rows, wide), (lambda i: (i, 0, 0))
    tile = pl.BlockSpec((high, wide), where)
    pair = pl.BlockSpec((2, high, wide), lambda i: (0,) + where(i))
    return pl.pallas_call(
        partial(adam_kernel, as_step),
        grid=grid,
        in_specs=[
            pl.BlockSpec(memory_space=pltpu.SMEM),
            tile,
            pair,
            pl.BlockSpec(grad_block, grad_where),
        ],
        out_specs=[tile, pair],
        out_shape=[
            jax.ShapeDtypeStruct(weight.shape, F32 if as_step else BF16),
            jax.ShapeDtypeStruct(moments.shape, F32),
        ],
        compiler_params=pltpu.CompilerParams(vmem_limit_bytes=VMEM_LIMIT),
        cost_estimate=pl.CostEstimate(
            flops=20 * weight.size, bytes_accessed=22 * weight.size, transcendentals=weight.size
        ),
    )(scalars, weight, moments, grad)


def column_sum(values):
    return jnp.sum(values.astype(F32), axis=0)


def body(
    tokens,
    cotangent,
    qkv_weight,
    out_weight,
    up_weight,
    down_weight,
    vectors,
    qkv_moments,
    out_moments,
    up_moments,
    down_moments,
    vector_moments,
    step,
    hyper,
):
    chip = lax.axis_index("chip")
    p = lax.axis_index(PLANE)
    devices = lax.axis_size(AXES)
    width = tokens.shape[2]
    place = jnp.stack([chip, lax.axis_index("z")]).astype(jnp.int32)
    heads = HEADS // GROUP
    head_ids = (p * heads + jnp.arange(heads)).astype(F32)
    slopes = jnp.exp2(-8.0 * (head_ids + 1.0) / HEADS)
    tokens_given, top_given = tokens[0], cotangent[0]

    flat = lax.axis_index(AXES)
    vecs = lax.dynamic_update_slice(
        jnp.zeros((vectors.shape[0], width), BF16), vectors, (0, flat * vectors.shape[1])
    )
    vecs = sum_all(vecs).astype(F32)
    held = trade(tokens_given, "chip").reshape(CHIPS, -1, width)
    held, qkv_weight = together(held, qkv_weight)
    pieces = to_planes(held)
    qkv_parts = trade_columns(qkv_weight, 3)
    pair_qkv = pair_up(qkv_parts, out_weight, True)
    pieces, pair_qkv = together(pieces, pair_qkv)
    full_qkv, full_out = gather_pair(pair_qkv, qkv_parts, out_weight, p, True)
    top_given, up_weight, pieces = together(top_given, up_weight, pieces)
    held_top = trade(top_given, "chip")
    up_parts = trade_columns(up_weight, 1)
    pieces, up_parts, held_top = together(pieces, up_parts, held_top)
    rows_in = jnp.concatenate(pieces, axis=0).astype(F32)
    normed, hat_one, factor_one = norm_forward(rows_in, vecs[0], vecs[1])
    normed_low, held_top = together(normed.astype(BF16), held_top)
    own = plane_order(normed_low)
    top_low = trade(held_top, "z")
    own, top_low, up_parts, w_qkv, w_out = together(own, top_low, up_parts, full_qkv, full_out)
    top_low = in_z_order(top_low)
    full_up = lax.all_gather(up_parts, ("o", "z"), axis=0, tiled=True)
    full_down = gather_rows(down_weight, p)
    own = jnp.concatenate(own, axis=0)
    own, top_low = together(own, top_low)
    normed_a = [own, swap_cores(own)]
    top_own = plane_order(top_low)
    part = width // GROUP
    bias_q = lax.dynamic_slice(vecs[2], (p * part,), (part,))
    bias_v = lax.dynamic_slice(vecs[3], (p * part,), (part,))
    bias_qkv = jnp.concatenate([bias_q, jnp.zeros_like(bias_q), bias_v])
    qkv = [(dot(v, w_qkv) + bias_qkv).astype(BF16) for v in normed_a]
    context = [attend(v, place, slopes) for v in qkv]
    context, top_own = together(context, top_own)
    top_own = jnp.concatenate(top_own, axis=0)
    term_other = dot(context[1], w_out).astype(BF16)
    term_own = dot(after(context[0], term_other), w_out).astype(BF16)
    pieces = chip_exchange(core_pieces(term_own, term_other))
    pieces, top_own, full_up = together(pieces, top_own, full_up)
    w_up = in_row_order(full_up, up_parts.shape[2])
    residual = rows_in + add_up(pieces) + vecs[4]
    normed, hat_two, factor_two = norm_forward(residual, vecs[5], vecs[6])
    normed_low = normed.astype(BF16)
    own = plane_order(normed_low)
    grad_mlp = [top_own, swap_cores(top_own)]
    own, grad_mlp, w_down, w_up = together(own, grad_mlp, full_down, w_up)
    own = jnp.concatenate(own, axis=0)
    normed_b = [own, swap_cores(own)]
    hidden_part = w_up.shape[1]
    bias_up = lax.dynamic_slice(vecs[8:].reshape(-1), (p * hidden_part,), (hidden_part,))

    hidden_other, grad_other, term_other = feed(normed_b[1], grad_mlp[1], w_up, w_down, bias_up)
    left, term_other = together(normed_b[0], term_other)
    hidden_own, grad_own, term_own = feed(left, grad_mlp[0], w_up, w_down, bias_up)
    hidden, grad_pre = [hidden_own, hidden_other], [grad_own, grad_other]
    pieces, held = together(core_pieces(term_own, term_other), hidden)
    grad_down = weight_grad(held, [grad_mlp])
    owned_down = scatter_rows(grad_down, p)
    pieces = chip_exchange(pieces)
    held, grad_down = together(grad_pre, grad_down)
    grad_up = weight_grad(normed_b, [held], up_weight.shape[0])
    pieces, grad_up = together(pieces, grad_up)
    grad_normed = add_up(pieces)
    through, gain_two_grad, shift_two_grad = norm_backward(grad_normed, hat_two, factor_two, vecs[5])
    grad_residual = top_low.astype(F32) + through
    grad_attn_own = grad_residual.astype(BF16)

    own = plane_order(grad_attn_own)
    held, grad_attn_own = together(hidden, grad_attn_own)
    mlp_other = dot(held[1], w_down).astype(BF16)
    mlp_own = dot(after(held[0], mlp_other), w_down).astype(BF16)
    reduced_up = scatter_columns(grad_up)
    mlp_sums = core_pieces(mlp_own, mlp_other)
    own = jnp.concatenate(own, axis=0)
    own, mlp_sums = together(own, mlp_sums)
    grad_attn = [own, swap_cores(own)]

    mlp_parts = chip_trade(mlp_sums, chip)
    grad_context = [dot_nt(v, w_out).astype(BF16) for v in grad_attn]
    grads = [attend_back(v, g, place, slopes) for v, g in zip(qkv, grad_context)]
    grads, owned_down = together(grads, owned_down)
    grad_qkv_weight = weight_grad(normed_a, list(zip(*grads)), qkv_weight.shape[0])
    held, grad_attn, grad_qkv_weight = together(context, grad_attn, grad_qkv_weight)
    grad_out = (dot_tn(held[0], grad_attn[0]) + dot_tn(held[1], grad_attn[1])).astype(BF16)
    grads, grad_out, mlp_parts = together(grads, grad_out, mlp_parts)
    term_other = terms(grads[1], w_qkv)
    result = (residual + sum_parts(mlp_parts) + vecs[7]).astype(BF16)
    held, term_other, reduced_up = together(grads[0], term_other, reduced_up)
    owned_up = trade_rows(reduced_up)
    owned_up, result = together(owned_up, result)
    result = trade(in_z_order(result), "z")
    term_own = terms(held, w_qkv)
    pieces = core_pieces(term_own, term_other)
    reduced_qkv, owned_out = scatter_pair(
        grad_qkv_weight, grad_out, qkv_weight.shape[0], p
    )
    pieces = chip_exchange(pieces)
    grads, grad_pre, pieces[1] = together(grads, grad_pre, pieces[1])
    pieces, owned_up, reduced_qkv, result = together(pieces, owned_up, reduced_qkv, result)
    grad_normed = add_up(pieces)
    through, gain_one_grad, shift_one_grad = norm_backward(grad_normed, hat_one, factor_one, vecs[0])
    owned_qkv = trade_rows(reduced_qkv)
    bias_grads = [column_sum(grads[0][i]) + column_sum(grads[1][i]) for i in (0, 2)]
    up_bias_grad = column_sum(grad_pre[0]) + column_sum(grad_pre[1])
    wide = lambda v: lax.dynamic_update_slice(jnp.zeros((width,), F32), v, (p * part,))
    up_wide = lax.dynamic_update_slice(
        jnp.zeros((GROUP * hidden_part,), F32), up_bias_grad, (p * hidden_part,)
    )
    vector_grad = jnp.concatenate(
        [
            jnp.stack(
                [
                    gain_one_grad,
                    shift_one_grad,
                    wide(bias_grads[0]),
                    wide(bias_grads[1]),
                    column_sum(grad_attn_own),
                    gain_two_grad,
                    shift_two_grad,
                    column_sum(top_given),
                ]
            ),
            up_wide.reshape(-1, width),
        ],
        axis=0,
    )
    vec_parts = vector_grad.reshape(vectors.shape[0], devices, -1).transpose(1, 0, 2)
    vec_parts, owned_qkv = together(vec_parts, owned_qkv)
    owned_vec = jnp.sum(trade(vec_parts, AXES), axis=0)

    grad_qkv_rows = owned_qkv.reshape(GROUP, -1, 3, part).transpose(1, 2, 0, 3).reshape(qkv_weight.shape)
    squares = [jnp.sum(jnp.square(g.astype(F32))) for g in (grad_qkv_rows, owned_out, owned_up, owned_down, owned_vec)]
    squares = jnp.broadcast_to(sum(squares), (devices, 1))
    grad_norm = jnp.sqrt(jnp.sum(trade(squares, AXES)))
    back = (grad_residual + through).astype(BF16)
    back = from_planes(back)
    back, grad_norm = together(back, grad_norm)
    result, back = together(result, by_chip(back))
    both = trade(jnp.concatenate([result, back], axis=1), "chip")
    clip_factor = jnp.minimum(1.0, hyper[4] / (grad_norm + 1e-06))
    step_float = step.astype(F32)
    fix_first = 1.0 / (1.0 - hyper[2] ** step_float)
    fix_second = 1.0 / (1.0 - hyper[3] ** step_float)
    scalars = [clip_factor, hyper[2], hyper[3], fix_first, fix_second, hyper[0], hyper[1]]
    listed = jnp.stack(scalars)
    new_qkv, new_qkv_moments = adam_update(qkv_weight, qkv_moments, grad_qkv_rows, listed)
    out_step, new_out_moments = adam_update(out_weight, out_moments, owned_out, listed, as_step=True)
    new_up, new_up_moments = adam_update(up_weight, up_moments, owned_up, listed)
    new_down, new_down_moments = adam_update(down_weight, down_moments, owned_down, listed)
    both, new_qkv, out_step, new_up, new_down = together(both, new_qkv, out_step, new_up, new_down)
    activations, input_grad = both[:, :width], both[:, width:]
    first, second, vector_step = adam_step(
        vectors.astype(F32), vector_moments[0], vector_moments[1], owned_vec, scalars
    )
    return (
        activations[None],
        input_grad[None],
        grad_norm,
        new_qkv,
        out_step,
        new_up,
        new_down,
        vector_step,
        new_qkv_moments,
        new_out_moments,
        new_up_moments,
        new_down_moments,
        jnp.stack([first, second]),
    )


def solution(mesh):
    devices = np.asarray(mesh.devices)
    planes = Mesh(devices.reshape(-1, CHIPS, 2, devices.shape[1]), AXES)
    rows = P(AXES, None)
    seqs = P(("o",) + PLANE, "z", None)
    pair = P(None, AXES, None)
    cols = P(None, AXES)
    return jax.shard_map(
        body,
        mesh=planes,
        in_specs=(seqs, seqs, rows, rows, rows, rows, cols)
        + (pair, pair, pair, pair, P(None, None, AXES), P(), P()),
        out_specs=(seqs, seqs, P(), rows, rows, rows, rows, cols)
        + (pair, pair, pair, pair, P(None, None, AXES)),
        check_vma=False,
    )
```

```python
from functools import partial

import jax
import jax.numpy as jnp
import numpy as np
from jax import lax
from jax.experimental import pallas as pl
from jax.experimental.pallas import tpu as pltpu
from jax.sharding import Mesh
from jax.sharding import PartitionSpec as P

HEADS = 16
HEAD_DIM = 128
GROUP = 8
CHIPS = GROUP // 2

EPS_NORM = 1e-05
EPS_ADAM = 1e-08
F32 = jnp.float32
BF16 = jnp.bfloat16
PLANE = ("chip", "core")
AXES = ("o",) + PLANE + ("z",)
VMEM_LIMIT = 56 * 1024 * 1024


def after(value, *others):
    return lax.optimization_barrier((value,) + others)[0]


def together(*values):
    return lax.optimization_barrier(values)


def dot(a, b):
    return jnp.dot(a, b, preferred_element_type=F32)


def dot_nt(a, b):
    return lax.dot_general(a, b, (((1,), (1,)), ((), ())), preferred_element_type=F32)


def dot_tn(a, b):
    return lax.dot_general(a, b, (((0,), (0,)), ((), ())), preferred_element_type=F32)


def swap_chips(value, k):
    return lax.ppermute(value, "chip", [(q, q ^ k) for q in range(CHIPS)])


def swap_cores(value):
    return lax.ppermute(value, "core", [(0, 1), (1, 0)])


def swap(value, axis, k):
    return lax.ppermute(value, axis, [(i, i ^ k) for i in range(lax.axis_size(axis))])


def sum_all(value):
    for axis in AXES:
        k = 1
        while k < lax.axis_size(axis):
            value = value + swap(value, axis, k)
            k *= 2
    return value


def trade(value, axes):
    return lax.all_to_all(value, axes, 0, 0, tiled=True)


def pick(stacked, index):
    return lax.dynamic_index_in_dim(stacked, index, 0, keepdims=False)


def plane_order(own):
    return [own] + [swap_chips(own, k) for k in range(1, CHIPS)]


def to_planes(parts):
    z = lax.axis_index("z")
    return [pick(parts, z)] + [swap(pick(parts, z ^ k), "z", k) for k in range(1, CHIPS)]


def in_z_order(natural):
    z = lax.axis_index("z")
    parts = natural.reshape(CHIPS, -1, natural.shape[1])
    return jnp.concatenate([pick(parts, z ^ k) for k in range(CHIPS)], axis=0)


def from_planes(block):
    parts = block.reshape(CHIPS, -1, block.shape[1])
    return [parts[0]] + [swap(parts[k], "z", k) for k in range(1, CHIPS)]


def by_chip(pieces):
    z = lax.axis_index("z")
    held = jnp.stack(pieces)
    return jnp.concatenate([pick(held, z ^ q) for q in range(CHIPS)], axis=0)


def core_pieces(own_terms, other_terms):
    rows = own_terms.shape[0] // CHIPS
    arrived = swap_cores(other_terms)
    near = own_terms[:rows].astype(F32) + arrived[:rows].astype(F32)
    far = (own_terms[rows:].astype(F32) + arrived[rows:].astype(F32)).astype(BF16)
    return [near] + [far[k * rows : (k + 1) * rows] for k in range(CHIPS - 1)]


def chip_exchange(pieces):
    return pieces[:1] + [swap_chips(v, k) for k, v in enumerate(pieces) if k]


def add_up(pieces):
    return sum(v.astype(F32) for v in pieces)


def sum_parts(parts):
    return jnp.sum(parts.reshape(CHIPS, -1, parts.shape[1]).astype(F32), axis=0)


def chip_trade(pieces, chip):
    parts = jnp.stack([pieces[0].astype(BF16)] + pieces[1:])
    low = jnp.concatenate([pick(parts, chip ^ q) for q in range(CHIPS)], axis=0)
    return trade(low, "chip")


def trade_columns(weight, groups):
    rows, cols = weight.shape
    width = cols // (groups * GROUP)
    parts = weight.reshape(rows, groups, GROUP, width).transpose(2, 0, 1, 3)
    parts = parts.reshape(GROUP, rows, groups * width)
    return trade(parts, PLANE)


def side_by_side(stack, count):
    rows = stack.shape[0] // count
    return stack.reshape(count, rows, -1).transpose(1, 0, 2).reshape(rows, -1)


def stacked(wide, count):
    rows = wide.shape[0]
    return wide.reshape(rows, count, -1).transpose(1, 0, 2).reshape(count * rows, -1)


def in_row_order(full, width):
    o_size, z_size = lax.axis_size("o"), lax.axis_size("z")
    full = full.reshape(o_size, z_size, GROUP, -1, width).transpose(0, 2, 1, 3, 4)
    return full.reshape(-1, width)


def pair_up(parts, rows_weight, beside):
    width = parts.shape[2]
    flat = parts.reshape(-1, width)
    if lax.axis_size("o") > 1:
        return (flat, rows_weight)
    count = GROUP if beside else rows_weight.shape[1] // width
    return (jnp.concatenate([flat, after(stacked(rows_weight, count), ())], axis=1 if beside else 0),)


def gather_pair(pair, parts, rows_weight, p, beside):
    width = parts.shape[2]
    if len(pair) > 1:
        full = lax.all_gather(pair[0], ("o", "z"), axis=0, tiled=True)
        others = lax.all_gather(pair[1], AXES, axis=0, tiled=True)
        return in_row_order(full, width), pick(others.reshape(GROUP, -1, rows_weight.shape[1]), p)
    full = lax.all_gather(pair[0], "z", axis=0, tiled=False)
    first, second = jnp.split(full, [width if beside else parts.size // width], axis=2 if beside else 1)
    count = GROUP if beside else rows_weight.shape[1] // width
    second = [side_by_side(second[i], count) for i in range(full.shape[0])]
    return in_row_order(first, width), jnp.concatenate(second, axis=0)


def scatter_pair(grad_columns, grad_rows, rows, p):
    width = grad_columns.shape[1]
    if lax.axis_size("o") > 1:
        return scatter_columns(grad_columns), scatter_rows(grad_rows, p)
    z_size = lax.axis_size("z")
    beside = grad_rows.reshape(z_size, -1, grad_rows.shape[1])
    beside = after(jnp.concatenate([stacked(beside[i], GROUP) for i in range(z_size)], axis=0), ())
    both = jnp.concatenate([grad_columns, beside], axis=1)
    mine = lax.psum_scatter(both, "z", scatter_dimension=0, tiled=True)
    return mine[:, :width].reshape(GROUP, rows, width), side_by_side(mine[:, width:], GROUP)


def by_owner(grad, rows):
    o_size, z_size = lax.axis_size("o"), lax.axis_size("z")
    parts = grad.reshape(o_size, GROUP, z_size, rows, -1).transpose(0, 2, 1, 3, 4)
    return parts.reshape(grad.shape)


def scatter_columns(parts):
    mine = lax.psum_scatter(parts, ("o", "z"), scatter_dimension=0, tiled=True)
    return mine.reshape(GROUP, -1, parts.shape[1])


def trade_rows(parts):
    return trade(parts, PLANE)


def gather_rows(weight, p):
    if lax.axis_size("o") == 1:
        return lax.all_gather(weight, "z", axis=0, tiled=True)
    full = lax.all_gather(weight, AXES, axis=0, tiled=True)
    return pick(full.reshape(GROUP, -1, weight.shape[1]), p)


def scatter_rows(grad, p):
    if lax.axis_size("o") == 1:
        return lax.psum_scatter(grad, "z", scatter_dimension=0, tiled=True)
    full = jnp.zeros((GROUP,) + grad.shape, grad.dtype)
    full = lax.dynamic_update_index_in_dim(full, grad, p, 0)
    full = full.reshape(-1, grad.shape[1])
    return lax.psum_scatter(full, AXES, scatter_dimension=0, tiled=True)


def order_rows(pos_ref, blocks, rows):
    out = []
    for b in range(blocks):
        for q in range(CHIPS):
            held = ((q ^ pos_ref[0]) * blocks + (b ^ pos_ref[1])) * rows
            out.append(((b * CHIPS + q) * rows, pl.multiple_of(held, rows)))
    return out


def block_probs(q, keys, slope, start, scale):
    scores = dot_nt(q, keys) * scale
    row = lax.broadcasted_iota(jnp.int32, scores.shape, 0) + start
    col = lax.broadcasted_iota(jnp.int32, scores.shape, 1)
    scores = scores - slope * jnp.abs(row - col).astype(F32)
    expo = jnp.exp(scores - jnp.max(scores, axis=-1, keepdims=True))
    return expo * (1.0 / jnp.sum(expo, axis=-1, keepdims=True))


def attend_kernel(blocks, scale, pos_ref, slope_ref, q_ref, k_ref, v_ref, ctx_ref, qs, ks, vs):
    rows = q_ref.shape[0] // (blocks * CHIPS)
    block = rows * CHIPS
    slope = slope_ref[pl.program_id(0)]
    order = order_rows(pos_ref, blocks, rows)
    for nat, held in order:
        qs[nat : nat + rows] = q_ref[pl.ds(held, rows), :]
        ks[nat : nat + rows] = k_ref[pl.ds(held, rows), :]
        vs[nat : nat + rows] = v_ref[pl.ds(held, rows), :]
    for b in range(blocks):
        end = (b + 1) * block
        probs = block_probs(qs[b * block : end], ks[:end], slope, b * block, scale)
        ctx = dot(probs.astype(BF16), vs[:end]).astype(BF16)
        for q in range(CHIPS):
            held = order[b * CHIPS + q][1]
            ctx_ref[pl.ds(held, rows), :] = ctx[q * rows : (q + 1) * rows]


def attend_back_kernel(
    blocks, scale, pos_ref, slope_ref, q_ref, k_ref, v_ref, g_ref, gq_ref, gk_ref, gv_ref,
    qs, ks, vs, gs, gks, gvs,
):
    rows = q_ref.shape[0] // (blocks * CHIPS)
    block = rows * CHIPS
    slope = slope_ref[pl.program_id(0)]
    order = order_rows(pos_ref, blocks, rows)
    for nat, held in order:
        qs[nat : nat + rows] = q_ref[pl.ds(held, rows), :]
        ks[nat : nat + rows] = k_ref[pl.ds(held, rows), :]
        vs[nat : nat + rows] = v_ref[pl.ds(held, rows), :]
        gs[nat : nat + rows] = g_ref[pl.ds(held, rows), :]
    for b in reversed(range(blocks)):
        start, end = b * block, (b + 1) * block
        q, g = qs[start:end], gs[start:end]
        keys, values = ks[:end], vs[:end]
        probs = block_probs(q, keys, slope, start, scale)
        grad_values = dot_tn(probs.astype(BF16), g)
        grad_probs = dot_nt(g, values)
        inner = jnp.sum(probs * grad_probs, axis=-1, keepdims=True)
        grad_scores = (probs * (grad_probs - inner)).astype(BF16)
        grad_q = (dot(grad_scores, keys) * scale).astype(BF16)
        grad_keys = dot_tn(grad_scores, q)
        if b == blocks - 1:
            gks[...] = grad_keys
            gvs[...] = grad_values
        else:
            gks[:end] += grad_keys
            gvs[:end] += grad_values
        for c in range(CHIPS):
            held = order[b * CHIPS + c][1]
            gq_ref[pl.ds(held, rows), :] = grad_q[c * rows : (c + 1) * rows]
    for nat, held in order:
        gk_ref[pl.ds(held, rows), :] = (gks[nat : nat + rows] * scale).astype(BF16)
        gv_ref[pl.ds(held, rows), :] = gvs[nat : nat + rows].astype(BF16)


def attend(qkv, place, slopes):
    length, heads = qkv.shape[0], qkv.shape[1] // (3 * HEAD_DIM)
    blocks = lax.axis_size("z")
    smem = pl.BlockSpec(memory_space=pltpu.SMEM)
    column = lambda first: pl.BlockSpec((length, HEAD_DIM), lambda h: (0, first + h))
    held = pltpu.VMEM((length, HEAD_DIM), BF16)
    return pl.pallas_call(
        partial(attend_kernel, blocks, HEAD_DIM**-0.5),
        grid=(heads,),
        in_specs=[smem, smem, column(0), column(heads), column(2 * heads)],
        out_specs=column(0),
        out_shape=jax.ShapeDtypeStruct((length, heads * HEAD_DIM), BF16),
        scratch_shapes=[held] * 3,
        compiler_params=pltpu.CompilerParams(vmem_limit_bytes=VMEM_LIMIT),
        cost_estimate=pl.CostEstimate(
            flops=6 * length * length * HEAD_DIM * heads,
            bytes_accessed=16 * length * heads * HEAD_DIM,
            transcendentals=2 * length * length * heads,
        ),
    )(place, slopes, qkv, qkv, qkv)


def attend_back(qkv, grad_ctx, place, slopes):
    length, heads = qkv.shape[0], qkv.shape[1] // (3 * HEAD_DIM)
    blocks = lax.axis_size("z")
    smem = pl.BlockSpec(memory_space=pltpu.SMEM)
    column = lambda first: pl.BlockSpec((length, HEAD_DIM), lambda h: (0, first + h))
    held = pltpu.VMEM((length, HEAD_DIM), BF16)
    wide = pltpu.VMEM((length, HEAD_DIM), F32)
    return pl.pallas_call(
        partial(attend_back_kernel, blocks, HEAD_DIM**-0.5),
        grid=(heads,),
        in_specs=[smem, smem, column(0), column(heads), column(2 * heads), column(0)],
        out_specs=[column(0)] * 3,
        out_shape=[jax.ShapeDtypeStruct((length, heads * HEAD_DIM), BF16)] * 3,
        scratch_shapes=[held] * 4 + [wide] * 2,
        compiler_params=pltpu.CompilerParams(vmem_limit_bytes=VMEM_LIMIT),
        cost_estimate=pl.CostEstimate(
            flops=16 * length * length * HEAD_DIM * heads,
            bytes_accessed=28 * length * heads * HEAD_DIM,
            transcendentals=2 * length * length * heads,
        ),
    )(place, slopes, qkv, qkv, qkv, grad_ctx)


def feed_kernel(norm_ref, top_ref, up_ref, down_ref, bias_ref, hidden_ref, grad_ref, term_ref):
    pre = dot(norm_ref[...], up_ref[...]) + bias_ref[...]
    scale = (2.0 / np.pi) ** 0.5
    square = pre * pre
    bend = jnp.tanh(scale * (pre + 0.044715 * (pre * square)))
    cdf = 0.5 + 0.5 * bend
    hidden_ref[...] = (pre * cdf).astype(BF16)
    slope = cdf + (0.5 * scale) * pre * (1.0 - bend * bend) * (1.0 + (3.0 * 0.044715) * square)
    grad = (dot_nt(top_ref[...], down_ref[...]) * slope).astype(BF16)
    grad_ref[...] = grad
    term_ref[...] = dot_nt(grad, up_ref[...]).astype(BF16)


def feed(normed, top, w_up, w_down, bias):
    rows, width = normed.shape
    part = w_up.shape[1]
    tile = min(rows, 256)
    wide = pl.BlockSpec((tile, width), lambda i: (i, 0))
    slim = pl.BlockSpec((tile, part), lambda i: (i, 0))
    whole = lambda v: pl.BlockSpec(v.shape, lambda i: (0, 0))
    bias = bias.reshape(1, part)
    return pl.pallas_call(
        feed_kernel,
        grid=(rows // tile,),
        in_specs=[wide, wide, whole(w_up), whole(w_down), whole(bias)],
        out_specs=[slim, slim, wide],
        out_shape=[
            jax.ShapeDtypeStruct((rows, part), BF16),
            jax.ShapeDtypeStruct((rows, part), BF16),
            jax.ShapeDtypeStruct((rows, width), BF16),
        ],
        compiler_params=pltpu.CompilerParams(vmem_limit_bytes=VMEM_LIMIT),
        cost_estimate=pl.CostEstimate(
            flops=6 * rows * width * part,
            bytes_accessed=6 * rows * width + 4 * rows * part + 4 * width * part,
            transcendentals=rows * part,
        ),
    )(normed, top, w_up, w_down, bias)


def weight_kernel(count, left_0, left_1, *refs):
    rights, out_ref = refs[:-1], refs[-1]
    first = 0
    for i in range(count):
        a, b = rights[2 * i], rights[2 * i + 1]
        cols = a.shape[1]
        out = dot_tn(left_0[...], a[...]) + dot_tn(left_1[...], b[...])
        out_ref[..., first : first + cols] = out.astype(BF16).reshape(out_ref.shape[:-1] + (cols,))
        first += cols


def weight_grad(left, rights, owner_rows=None):
    rows, width = left[0].shape
    cols = sum(r[0].shape[1] for r in rights)
    if owner_rows and lax.axis_size("o") > 1:
        joined = [jnp.concatenate(v, axis=1) for v in zip(*rights)]
        grad = (dot_tn(left[0], joined[0]) + dot_tn(left[1], joined[1])).astype(BF16)
        return by_owner(grad, owner_rows)
    tile = 256
    if owner_rows:
        z_size = lax.axis_size("z")
        tile = z_size * owner_rows
        shape = (z_size, width // tile, owner_rows, cols)
        out_spec = pl.BlockSpec((z_size, 1, owner_rows, cols), lambda i: (0, i, 0, 0))
    else:
        shape = (width, cols)
        out_spec = pl.BlockSpec((tile, cols), lambda i: (i, 0))
    flat = [v for r in rights for v in r]
    out = pl.pallas_call(
        partial(weight_kernel, len(rights)),
        grid=(width // tile,),
        in_specs=[pl.BlockSpec((rows, tile), lambda i: (0, i))] * 2
        + [pl.BlockSpec(v.shape, lambda i: (0, 0)) for v in flat],
        out_specs=out_spec,
        out_shape=jax.ShapeDtypeStruct(shape, BF16),
        compiler_params=pltpu.CompilerParams(vmem_limit_bytes=VMEM_LIMIT),
        cost_estimate=pl.CostEstimate(
            flops=4 * rows * width * cols,
            bytes_accessed=4 * rows * (width + cols) + 2 * width * cols,
            transcendentals=0,
        ),
    )(*left, *flat)
    return out.reshape(width, cols)


def terms_kernel(*refs):
    weight_ref, out_ref = refs[-2:]
    total, first = 0.0, 0
    for ref in refs[:-2]:
        total = total + dot_nt(ref[...], weight_ref[:, first : first + ref.shape[1]])
        first += ref.shape[1]
    out_ref[...] = total.astype(BF16)


def terms(lefts, weight):
    rows, width = lefts[0].shape[0], weight.shape[0]
    tile = min(rows, 256)
    return pl.pallas_call(
        terms_kernel,
        grid=(rows // tile,),
        in_specs=[pl.BlockSpec((tile, v.shape[1]), lambda i: (i, 0)) for v in lefts]
        + [pl.BlockSpec(weight.shape, lambda i: (0, 0))],
        out_specs=pl.BlockSpec((tile, width), lambda i: (i, 0)),
        out_shape=jax.ShapeDtypeStruct((rows, width), BF16),
        compiler_params=pltpu.CompilerParams(vmem_limit_bytes=VMEM_LIMIT),
        cost_estimate=pl.CostEstimate(
            flops=2 * rows * weight.size,
            bytes_accessed=2 * weight.size + 4 * rows * width,
            transcendentals=0,
        ),
    )(*lefts, weight)


def norm_forward(values, gain, shift):
    centre = values - jnp.mean(values, axis=-1, keepdims=True)
    factor = lax.rsqrt(jnp.mean(centre * centre, axis=-1, keepdims=True) + EPS_NORM)
    normed = centre * factor
    return (normed * gain + shift, normed, factor)


def norm_backward(incoming, normed, factor, gain):
    scaled = incoming * gain
    input_grad = factor * (
        scaled
        - jnp.mean(scaled, axis=-1, keepdims=True)
        - normed * jnp.mean(scaled * normed, axis=-1, keepdims=True)
    )
    return (input_grad, jnp.sum(incoming * normed, axis=0), jnp.sum(incoming, axis=0))


def adam_step(weight, first, second, grad, scalars):
    clip, keep_first, keep_second, fix_first, fix_second, rate, decay = scalars
    scaled = grad * clip
    first = keep_first * first + (1.0 - keep_first) * scaled
    second = keep_second * second + (1.0 - keep_second) * scaled * scaled
    change = -rate * (
        first * fix_first / (jnp.sqrt(second * fix_second) + EPS_ADAM) + decay * weight
    )
    return first, second, change


def adam_kernel(as_step, scalar_ref, weight_ref, moment_ref, grad_ref, out_ref, new_ref):
    scalars = [scalar_ref[i] for i in range(7)]
    weight = weight_ref[...].astype(F32)
    grad = grad_ref[...].reshape(weight.shape).astype(F32)
    first, second, change = adam_step(weight, moment_ref[0], moment_ref[1], grad, scalars)
    new_ref[0] = first
    new_ref[1] = second
    out_ref[...] = change if as_step else (weight + change).astype(BF16)


def adam_update(weight, moments, grad, scalars, as_step=False):
    rows, cols = weight.shape
    if grad.ndim == 2:
        high, wide = (16 if cols > 4096 else max(16, rows // 4)), cols
        grid, where, grad_block, grad_where = (rows // high,), (lambda i: (i, 0)), (high, wide), (lambda i: (i, 0))
    else:
        high, wide = rows, grad.shape[2]
        grid, where, grad_block, grad_where = (GROUP,), (lambda i: (0, i)), (1, rows, wide), (lambda i: (i, 0, 0))
    tile = pl.BlockSpec((high, wide), where)
    pair = pl.BlockSpec((2, high, wide), lambda i: (0,) + where(i))
    return pl.pallas_call(
        partial(adam_kernel, as_step),
        grid=grid,
        in_specs=[
            pl.BlockSpec(memory_space=pltpu.SMEM),
            tile,
            pair,
            pl.BlockSpec(grad_block, grad_where),
        ],
        out_specs=[tile, pair],
        out_shape=[
            jax.ShapeDtypeStruct(weight.shape, F32 if as_step else BF16),
            jax.ShapeDtypeStruct(moments.shape, F32),
        ],
        compiler_params=pltpu.CompilerParams(vmem_limit_bytes=VMEM_LIMIT),
        cost_estimate=pl.CostEstimate(
            flops=20 * weight.size, bytes_accessed=22 * weight.size, transcendentals=weight.size
        ),
    )(scalars, weight, moments, grad)


def column_sum(values):
    return jnp.sum(values.astype(F32), axis=0)


def body(
    tokens,
    cotangent,
    qkv_weight,
    out_weight,
    up_weight,
    down_weight,
    vectors,
    qkv_moments,
    out_moments,
    up_moments,
    down_moments,
    vector_moments,
    step,
    hyper,
):
    chip = lax.axis_index("chip")
    p = lax.axis_index(PLANE)
    devices = lax.axis_size(AXES)
    width = tokens.shape[2]
    place = jnp.stack([chip, lax.axis_index("z")]).astype(jnp.int32)
    heads = HEADS // GROUP
    head_ids = (p * heads + jnp.arange(heads)).astype(F32)
    slopes = jnp.exp2(-8.0 * (head_ids + 1.0) / HEADS)
    tokens_given, top_given = tokens[0], cotangent[0]

    flat = lax.axis_index(AXES)
    vecs = lax.dynamic_update_slice(
        jnp.zeros((vectors.shape[0], width), BF16), vectors, (0, flat * vectors.shape[1])
    )
    vecs = sum_all(vecs).astype(F32)
    held = trade(tokens_given, "chip").reshape(CHIPS, -1, width)
    held, qkv_weight = together(held, qkv_weight)
    pieces = to_planes(held)
    qkv_parts = trade_columns(qkv_weight, 3)
    pair_qkv = pair_up(qkv_parts, out_weight, True)
    pieces, pair_qkv = together(pieces, pair_qkv)
    full_qkv, full_out = gather_pair(pair_qkv, qkv_parts, out_weight, p, True)
    top_given, up_weight, pieces = together(top_given, up_weight, pieces)
    held_top = trade(top_given, "chip")
    up_parts = trade_columns(up_weight, 1)
    pieces, up_parts, held_top = together(pieces, up_parts, held_top)
    rows_in = jnp.concatenate(pieces, axis=0).astype(F32)
    normed, hat_one, factor_one = norm_forward(rows_in, vecs[0], vecs[1])
    normed_low, held_top = together(normed.astype(BF16), held_top)
    own = plane_order(normed_low)
    top_low = trade(held_top, "z")
    own, top_low, up_parts, w_qkv, w_out = together(own, top_low, up_parts, full_qkv, full_out)
    top_low = in_z_order(top_low)
    full_up = lax.all_gather(up_parts, ("o", "z"), axis=0, tiled=True)
    full_down = gather_rows(down_weight, p)
    own = jnp.concatenate(own, axis=0)
    own, top_low = together(own, top_low)
    normed_a = [own, swap_cores(own)]
    top_own = plane_order(top_low)
    part = width // GROUP
    bias_q = lax.dynamic_slice(vecs[2], (p * part,), (part,))
    bias_v = lax.dynamic_slice(vecs[3], (p * part,), (part,))
    bias_qkv = jnp.concatenate([bias_q, jnp.zeros_like(bias_q), bias_v])
    qkv = [(dot(v, w_qkv) + bias_qkv).astype(BF16) for v in normed_a]
    context = [attend(v, place, slopes) for v in qkv]
    context, top_own = together(context, top_own)
    top_own = jnp.concatenate(top_own, axis=0)
    term_other = dot(context[1], w_out).astype(BF16)
    term_own = dot(after(context[0], term_other), w_out).astype(BF16)
    pieces = chip_exchange(core_pieces(term_own, term_other))
    pieces, top_own, full_up = together(pieces, top_own, full_up)
    w_up = in_row_order(full_up, up_parts.shape[2])
    residual = rows_in + add_up(pieces) + vecs[4]
    normed, hat_two, factor_two = norm_forward(residual, vecs[5], vecs[6])
    normed_low = normed.astype(BF16)
    own = plane_order(normed_low)
    grad_mlp = [top_own, swap_cores(top_own)]
    own, grad_mlp, w_down, w_up = together(own, grad_mlp, full_down, w_up)
    own = jnp.concatenate(own, axis=0)
    normed_b = [own, swap_cores(own)]
    hidden_part = w_up.shape[1]
    bias_up = lax.dynamic_slice(vecs[8:].reshape(-1), (p * hidden_part,), (hidden_part,))

    hidden_other, grad_other, term_other = feed(normed_b[1], grad_mlp[1], w_up, w_down, bias_up)
    left, term_other = together(normed_b[0], term_other)
    hidden_own, grad_own, term_own = feed(left, grad_mlp[0], w_up, w_down, bias_up)
    hidden, grad_pre = [hidden_own, hidden_other], [grad_own, grad_other]
    pieces, held = together(core_pieces(term_own, term_other), hidden)
    grad_down = weight_grad(held, [grad_mlp])
    owned_down = scatter_rows(grad_down, p)
    pieces = chip_exchange(pieces)
    held, grad_down = together(grad_pre, grad_down)
    grad_up = weight_grad(normed_b, [held], up_weight.shape[0])
    pieces, grad_up = together(pieces, grad_up)
    grad_normed = add_up(pieces)
    through, gain_two_grad, shift_two_grad = norm_backward(grad_normed, hat_two, factor_two, vecs[5])
    grad_residual = top_low.astype(F32) + through
    grad_attn_own = grad_residual.astype(BF16)

    own = plane_order(grad_attn_own)
    held, grad_attn_own = together(hidden, grad_attn_own)
    mlp_other = dot(held[1], w_down).astype(BF16)
    mlp_own = dot(after(held[0], mlp_other), w_down).astype(BF16)
    reduced_up = scatter_columns(grad_up)
    mlp_sums = core_pieces(mlp_own, mlp_other)
    own = jnp.concatenate(own, axis=0)
    own, mlp_sums = together(own, mlp_sums)
    grad_attn = [own, swap_cores(own)]

    mlp_parts = chip_trade(mlp_sums, chip)
    grad_context = [dot_nt(v, w_out).astype(BF16) for v in grad_attn]
    grads = [attend_back(v, g, place, slopes) for v, g in zip(qkv, grad_context)]
    grads, owned_down = together(grads, owned_down)
    grad_qkv_weight = weight_grad(normed_a, list(zip(*grads)), qkv_weight.shape[0])
    held, grad_attn, grad_qkv_weight = together(context, grad_attn, grad_qkv_weight)
    grad_out = (dot_tn(held[0], grad_attn[0]) + dot_tn(held[1], grad_attn[1])).astype(BF16)
    grads, grad_out, mlp_parts = together(grads, grad_out, mlp_parts)
    term_other = terms(grads[1], w_qkv)
    held, term_other, reduced_up = together(grads[0], term_other, reduced_up)
    term_own = terms(held, w_qkv)
    pieces = core_pieces(term_own, term_other)
    reduced_qkv, owned_out = scatter_pair(
        grad_qkv_weight, grad_out, qkv_weight.shape[0], p
    )
    pieces, mlp_parts, reduced_up = together(pieces, mlp_parts, reduced_up)
    pieces = chip_exchange(pieces)
    owned_up = trade_rows(reduced_up)
    result = (residual + sum_parts(mlp_parts) + vecs[7]).astype(BF16)
    grads, grad_pre, pieces[1] = together(grads, grad_pre, pieces[1])
    pieces, result = together(pieces, result)
    grad_normed = add_up(pieces)
    through, gain_one_grad, shift_one_grad = norm_backward(grad_normed, hat_one, factor_one, vecs[0])
    bias_grads = [column_sum(grads[0][i]) + column_sum(grads[1][i]) for i in (0, 2)]
    up_bias_grad = column_sum(grad_pre[0]) + column_sum(grad_pre[1])
    wide = lambda v: lax.dynamic_update_slice(jnp.zeros((width,), F32), v, (p * part,))
    up_wide = lax.dynamic_update_slice(
        jnp.zeros((GROUP * hidden_part,), F32), up_bias_grad, (p * hidden_part,)
    )
    vector_grad = jnp.concatenate(
        [
            jnp.stack(
                [
                    gain_one_grad,
                    shift_one_grad,
                    wide(bias_grads[0]),
                    wide(bias_grads[1]),
                    column_sum(grad_attn_own),
                    gain_two_grad,
                    shift_two_grad,
                    column_sum(top_given),
                ]
            ),
            up_wide.reshape(-1, width),
        ],
        axis=0,
    )
    vec_parts = vector_grad.reshape(vectors.shape[0], devices, -1).transpose(1, 0, 2)
    vec_parts, reduced_qkv, owned_up = together(vec_parts, reduced_qkv, owned_up)
    owned_qkv = trade_rows(reduced_qkv)
    owned_vec = jnp.sum(trade(vec_parts, AXES), axis=0)

    grad_qkv_rows = owned_qkv.reshape(GROUP, -1, 3, part).transpose(1, 2, 0, 3).reshape(qkv_weight.shape)
    squares = [jnp.sum(jnp.square(g.astype(F32))) for g in (grad_qkv_rows, owned_out, owned_up, owned_down, owned_vec)]
    squares = jnp.broadcast_to(sum(squares), (devices, 1))
    grad_norm = jnp.sqrt(jnp.sum(trade(squares, AXES)))
    back = (grad_residual + through).astype(BF16)
    result, back = from_planes(result), from_planes(back)
    clip_factor = jnp.minimum(1.0, hyper[4] / (grad_norm + 1e-06))
    step_float = step.astype(F32)
    fix_first = 1.0 / (1.0 - hyper[2] ** step_float)
    fix_second = 1.0 / (1.0 - hyper[3] ** step_float)
    scalars = [clip_factor, hyper[2], hyper[3], fix_first, fix_second, hyper[0], hyper[1]]
    listed = jnp.stack(scalars)
    new_qkv, new_qkv_moments = adam_update(qkv_weight, qkv_moments, grad_qkv_rows, listed)
    out_step, new_out_moments = adam_update(out_weight, out_moments, owned_out, listed, as_step=True)
    result, back, new_qkv, out_step, listed = together(result, back, new_qkv, out_step, listed)
    result, back = together(by_chip(result), by_chip(back))
    both = trade(jnp.concatenate([result, back], axis=1), "chip")
    new_up, new_up_moments = adam_update(up_weight, up_moments, owned_up, listed)
    new_down, new_down_moments = adam_update(down_weight, down_moments, owned_down, listed)
    both, new_qkv, out_step, new_up, new_down = together(both, new_qkv, out_step, new_up, new_down)
    activations, input_grad = both[:, :width], both[:, width:]
    first, second, vector_step = adam_step(
        vectors.astype(F32), vector_moments[0], vector_moments[1], owned_vec, scalars
    )
    return (
        activations[None],
        input_grad[None],
        grad_norm,
        new_qkv,
        out_step,
        new_up,
        new_down,
        vector_step,
        new_qkv_moments,
        new_out_moments,
        new_up_moments,
        new_down_moments,
        jnp.stack([first, second]),
    )


def solution(mesh):
    devices = np.asarray(mesh.devices)
    planes = Mesh(devices.reshape(-1, CHIPS, 2, devices.shape[1]), AXES)
    rows = P(AXES, None)
    seqs = P(("o",) + PLANE, "z", None)
    pair = P(None, AXES, None)
    cols = P(None, AXES)
    return jax.shard_map(
        body,
        mesh=planes,
        in_specs=(seqs, seqs, rows, rows, rows, rows, cols)
        + (pair, pair, pair, pair, P(None, None, AXES), P(), P()),
        out_specs=(seqs, seqs, P(), rows, rows, rows, rows, cols)
        + (pair, pair, pair, pair, P(None, None, AXES)),
        check_vma=False,
    )
```
